256 devices in a mesh: dp: 2 (over z_lo), fsdp: 128 (over z_hi, x, y, core).
Axes of the slice: x: 4, y: 4, z: 8 (z_hi: 4, z_lo: 2; z = z_hi * 2 + z_lo), core: 2. Of those that a mesh axis runs over, the one named last changes fastest.
Arguments:
- output_gradient: bfloat16 [1024, 16384], P('dp', 'fsdp'), may hold values from -6 to 6
- gate_preactivation: bfloat16 [1024, 32768], P('dp', 'fsdp'), may hold values from -6 to 6
- up_preactivation: bfloat16 [1024, 32768], P('dp', 'fsdp'), may hold values from -6 to 6
- down_packed_codes: int32 [32768, 8192], P('fsdp'), may hold values from 0 to 255
- down_group_scales: float32 [256, 16384], P('fsdp'), may hold values from 0.0002762136 to 0.0022097088
- down_zero_points: int32 [256, 16384], P('fsdp'), may hold values from 0 to 15
- adapter_input_map: bfloat16 [16, 32768], P(None, 'fsdp'), may hold values from -0.5 to 0.5
- adapter_output_map: bfloat16 [16, 16384], P(None, 'fsdp'), may hold values from -0.046875 to 0.046875
Outputs:
- gate_gradient: bfloat16 [1024, 32768], P('dp', 'fsdp')
- up_gradient: bfloat16 [1024, 32768], P('dp', 'fsdp')
- adapter_input_gradient: float32 [16, 32768], P(None, 'fsdp')
- adapter_output_gradient: float32 [16, 16384], P(None, 'fsdp')
The draws below stay inside these ranges and needn't reach their ends.
Inputs may be any that keep to these rules, and one draw needn't show every extreme that they name: `down_packed_codes`: each word holds the code of feature d in bits 0 to 3 and that of feature d + 8192 in bits 4 to 7.
All inputs are finite; a program needn't handle non-finite values.
Results may differ from the reference program's by a relative error of at most 0.0051.
Values may be sent and summed in bfloat16 or wider, within the bound.
A program may use at most 128 MiB of HBM per device.

```python
import math
import jax
import jax.numpy as jnp
from jax import lax

MODEL_WIDTH = 16384
GROUP = 128
ADAPTER_RANK = 16
HIDDEN_COUNT = 32768
TOKEN_COUNT = 1024


def plant(values, rng, low, top_value):
    extent = values.shape
    index_at = [jax.random.randint(jax.random.fold_in(rng, axis), (), 0, extent[axis]) for axis in range(len(extent))]
    values = values.at[tuple(index_at)].set(low)
    longest = extent.index(max(extent))
    index_at[longest] = (index_at[longest] + 1) % extent[longest]
    return values.at[tuple(index_at)].set(top_value)


def shard_levels(rng, extent, cuts, least, high):
    def one(axis_at, parts):
        draws = jax.random.uniform(jax.random.fold_in(jax.random.fold_in(rng, 6), axis_at), (parts,), jnp.float32, least / len(cuts), high / len(cuts))
        return jnp.repeat(jnp.exp(draws), extent[axis_at] // parts).reshape((-1,) + (1,) * (len(extent) - axis_at - 1))

    level = one(*cuts[0])
    for cut in cuts[1:]:
        level = level * one(*cut)
    return level


def gaussian(key, extent, width, reach, cuts=(), dtype=jnp.bfloat16):
    result = width * jax.random.normal(key, extent, jnp.float32)
    if cuts:
        result = result * shard_levels(key, extent, cuts, -0.22, 0.18)
    return jnp.clip(result, -reach, reach).astype(dtype)


def setup_inputs(seed: int = 0) -> dict:
    streams_of = jax.random.split(jax.random.key(seed), 9)
    return {
        "output_gradient": gaussian(streams_of[0], (TOKEN_COUNT, MODEL_WIDTH), 1.0, 6.0, ((0, 2), (1, 128))),
        "gate_preactivation": gaussian(streams_of[1], (TOKEN_COUNT, HIDDEN_COUNT), 1.0, 6.0, ((0, 2), (1, 128))),
        "up_preactivation": gaussian(streams_of[2], (TOKEN_COUNT, HIDDEN_COUNT), 1.0, 6.0, ((0, 2), (1, 128))),
        "down_packed_codes": plant(jax.random.randint(streams_of[3], (HIDDEN_COUNT, MODEL_WIDTH // 2), 0, 256), jax.random.fold_in(streams_of[3], 1), 0, 255).astype(jnp.int32),
        "down_group_scales": jnp.clip(jnp.exp(math.log(0.0022097088) - 2.0794415 * jax.random.uniform(streams_of[4], (HIDDEN_COUNT // GROUP, MODEL_WIDTH), jnp.float32) ** shard_levels(streams_of[4], (HIDDEN_COUNT // GROUP, MODEL_WIDTH), ((0, 128),), -0.2, 0.2)), 0.0002762136, 0.0022097088),
        "down_zero_points": plant(jax.random.randint(streams_of[5], (HIDDEN_COUNT // GROUP, MODEL_WIDTH), 0, 16), jax.random.fold_in(streams_of[5], 1), 0, 15).astype(jnp.int32),
        "adapter_input_map": gaussian(streams_of[6], (ADAPTER_RANK, HIDDEN_COUNT), 128 ** -0.5, 0.5, ((1, 128),)),
        "adapter_output_map": gaussian(streams_of[7], (ADAPTER_RANK, MODEL_WIDTH), MODEL_WIDTH ** -0.5, 0.046875, ((1, 128),)),
    }


adapter_scale = 2.0


def dequantize(codes, scales, zeros, group):
    rows = codes.shape[0]
    half = codes.shape[1]
    lower = jnp.bitwise_and(codes, 15)
    upper = jnp.bitwise_and(jnp.right_shift(codes, 4), 15)
    levels = jnp.concatenate([lower, upper], axis=1).reshape(rows // group, group, 2 * half)
    values = scales[:, None, :] * (levels - zeros[:, None, :]).astype(jnp.float32)
    return values.reshape(rows, 2 * half).astype(jnp.bfloat16)


def reference(output_gradient, gate_preactivation, up_preactivation, down_packed_codes, down_group_scales, down_zero_points, adapter_input_map, adapter_output_map):
    def block_rows(items):
        codes, scales, zeros = items
        weight = dequantize(codes, scales[None, :], zeros[None, :], GROUP)
        return jnp.dot(output_gradient, weight.T, preferred_element_type=jnp.float32)

    pieces = lax.map(block_rows, (down_packed_codes.reshape(HIDDEN_COUNT // GROUP, GROUP, MODEL_WIDTH // 2), down_group_scales, down_zero_points))
    frozen_path_gradient = jnp.transpose(pieces, (1, 0, 2)).reshape(TOKEN_COUNT, HIDDEN_COUNT)
    gate_f = gate_preactivation.astype(jnp.float32)
    up_f = up_preactivation.astype(jnp.float32)
    sigma = jax.nn.sigmoid(gate_f)
    hidden_units = (gate_f * sigma * up_f).astype(jnp.bfloat16)
    left_operand = jnp.dot(hidden_units, adapter_input_map.T, preferred_element_type=jnp.float32)
    right_operand = jnp.dot(output_gradient, adapter_output_map.T, preferred_element_type=jnp.float32)
    left_lower_nibble = left_operand.astype(jnp.bfloat16)
    right_lower_nibble = right_operand.astype(jnp.bfloat16)
    hidden_gradient = frozen_path_gradient + adapter_scale * jnp.dot(right_lower_nibble, adapter_input_map, preferred_element_type=jnp.float32)
    up_gradient = (hidden_gradient * gate_f * sigma).astype(jnp.bfloat16)
    gate_gradient = (hidden_gradient * up_f * sigma * (1.0 + gate_f * (1.0 - sigma))).astype(jnp.bfloat16)
    scale_factor = adapter_scale / TOKEN_COUNT
    adapter_input_gradient = scale_factor * jnp.dot(right_lower_nibble.T, hidden_units, preferred_element_type=jnp.float32)
    adapter_output_gradient = scale_factor * jnp.dot(left_lower_nibble.T, output_gradient, preferred_element_type=jnp.float32)
    return gate_gradient, up_gradient, adapter_input_gradient, adapter_output_gradient
```

```python
import functools

import jax
import jax.numpy as jnp
from jax import lax
from jax.experimental import pallas as pl
from jax.experimental.pallas import tpu as pltpu
from jax.sharding import PartitionSpec as P

MESH = pl.DeviceIdType.MESH
F32 = jnp.float32
BF16 = jnp.bfloat16
SCALE = 2.0
LAG1, LAG2, LAG_OWN, LAG_SIB = 2, 4, 5, 6
STEPS = 16
NT = (((1,), (1,)), ((), ()))
TN = (((0,), (0,)), ((), ()))


def kernel(
    tokens,
    og, gate, up, codes, scales, zeros, amap, omap,
    gate_out, up_out, ain_out, aout_out,
    buf, w, cbuf, sc_v, ze_v, gate_v, up_v, am_v, om_v, og_v,
    hid, f1, f2, acc, gres, ures,
    p_src, p_dst, r0, s1, s2, s3, s4, fin, ad_mine, ad_peer, ad_sum,
    load_sem, code_sem, local_sem, ssem, sib_ssem, rsem, sib_rsem, own_rsem, small_ssem, small_rsem, out_sem,
):
    dp = lax.axis_index("dp")
    f = lax.axis_index("fsdp")
    c = lax.rem(f, 2)
    y = lax.rem(lax.div(f, 2), 4)
    x = lax.rem(lax.div(f, 8), 4)
    z = lax.div(f, 32)
    a = y + c * (x - y)
    b = x + c * (y - x)
    o = 1 - c

    def chip(px, py, pz, core):
        return (dp, ((pz * 4 + px) * 4 + py) * 2 + core)

    def neighbour(da, dz, db):
        pa, pz, pb = lax.rem(a + da, 4), lax.rem(z + dz, 4), lax.rem(b + db, 4)
        return chip(pb + c * (pa - pb), pa + c * (pb - pa), pz, c)

    sibling = (dp, f + 1 - 2 * c)
    partner = (1 - dp, f)

    def slot(da, dz, db):
        return lax.rem(z + dz, 4) * 16 + lax.rem(a + da, 4) * 4 + lax.rem(b + db, 4)

    def rel(da, dz, db):
        return lax.rem(dz + 4, 4) * 16 + lax.rem(da + 4, 4) * 4 + lax.rem(db + 4, 4)

    def irel(da, dz, db):
        return ((dz % 4) * 4 + da % 4) * 4 + db % 4

    me = slot(0, 0, 0)
    me_other = z * 16 + b * 4 + a

    loads = [
        pltpu.make_async_copy(s, d, load_sem.at[i])
        for i, (s, d) in enumerate(
            ((og, og_v), (gate, gate_v), (up, up_v), (amap, am_v), (omap, om_v), (scales, sc_v), (zeros, ze_v))
        )
    ]
    for load in loads:
        load.start()

    def code_load(ch):
        return pltpu.make_async_copy(
            codes.at[:, pl.ds(pl.multiple_of(ch * 1024, 1024), 1024)], cbuf.at[ch], code_sem.at[ch]
        )

    for ch in range(8):
        code_load(ch).start()

    bar = pltpu.get_barrier_semaphore()
    peers = [neighbour(1, 0, 0), neighbour(2, 0, 0), neighbour(3, 0, 0)]
    peers += [neighbour(0, 1, 0), neighbour(0, 2, 0), neighbour(0, 3, 0)]
    peers += [neighbour(0, 0, 1), neighbour(0, 0, 2), neighbour(0, 0, 3)]
    peers += [sibling, partner]
    for peer in peers:
        pl.semaphore_signal(bar, inc=1, device_id=peer, device_id_type=MESH)

    for load in loads[:5]:
        load.wait()
    for h in range(2):
        rows = pl.ds(h * 256, 256)
        g = gate_v[rows, :].astype(F32)
        u = up_v[rows, :].astype(F32)
        sig = 1.0 / (1.0 + jnp.exp(-g))
        silu = g * sig
        hid[rows, :] = (silu * u).astype(BF16)
        f1[rows, :] = silu
        f2[rows, :] = u * sig * (1.0 + g * (1.0 - sig))
        p_src[h, 0:16, :] = lax.dot_general(am_v[...], hid[rows, :], NT, preferred_element_type=F32)
        p_src[h, 16:32, :] = lax.dot_general(om_v[...], og_v[rows, :], NT, preferred_element_type=F32)
    acc[...] = jnp.zeros_like(acc)

    pl.semaphore_wait(bar, len(peers))

    def remote(src, dst, s_sem, r_sem, dev):
        return pltpu.make_async_remote_copy(
            src_ref=src, dst_ref=dst, send_sem=s_sem, recv_sem=r_sem, device_id=dev, device_id_type=MESH
        )

    def small(src, dst, i, dev):
        return remote(src, dst, small_ssem.at[i], small_rsem.at[i], dev)

    def own_rows(h):
        return og_v.at[pl.ds(pl.multiple_of(h * 256, 256), 256)]

    small(p_src.at[o], p_dst, 0, sibling).start()
    sib_own_c = remote(own_rows(c), buf.at[c, me, c], sib_ssem, own_rsem.at[0], sibling)
    sib_own_o = remote(own_rows(o), buf.at[o, me_other, c], sib_ssem, own_rsem.at[1], sibling)
    sib_own_o.start()
    hops = ((1, 0, 0), (3, 0, 0), (0, 1, 0), (0, 3, 0), (0, 0, 1), (0, 0, 3))

    def send_own(src, k):
        for da, dz, db in hops:
            remote(
                src, buf.at[c, me, k], ssem, rsem.at[irel(-da, -dz, -db) * 2 + k], neighbour(da, dz, db)
            ).start()

    send_own(own_rows(c), c)
    sib_own_c.start()
    local = [
        pltpu.make_async_copy(own_rows(c), buf.at[c, me, c], local_sem.at[0]),
        pltpu.make_async_copy(own_rows(o), buf.at[o, me_other, c], local_sem.at[1]),
    ]
    for copy in local:
        copy.start()
    remote(own_rows(o), buf.at[c, me, o], sib_ssem, own_rsem.at[1], sibling).wait_recv()
    send_own(buf.at[c, me, o], o)

    def wait_half(s, r, k):
        remote(buf.at[c, s, k], buf.at[c, s, k], ssem, rsem.at[r * 2 + k], sibling).wait_recv()

    def wait_whole(s, r):
        remote(buf.at[c, s], buf.at[c, s], ssem, rsem.at[r * 2], sibling).wait_recv()

    def wait_piece(s, r, split):
        @pl.when(split)
        def _():
            wait_half(s, r, 0)
            wait_half(s, r, 1)

        @pl.when(jnp.logical_not(split))
        def _():
            wait_whole(s, r)

    def send_whole(s, r, dev):
        remote(buf.at[c, s], buf.at[c, s], ssem, rsem.at[r * 2], dev).start()

    def send_half(s, k, r, dev):
        remote(buf.at[c, s, k], buf.at[c, s, k], ssem, rsem.at[r * 2 + k], dev).start()

    def send_sib(s, r):
        remote(buf.at[c, s], buf.at[c, s], sib_ssem, sib_rsem.at[r], sibling).start()

    b_up, b_down = neighbour(0, 0, 1), neighbour(0, 0, 3)
    z_up, z_down = neighbour(0, 1, 0), neighbour(0, 3, 0)
    a_up, a_down = neighbour(1, 0, 0), neighbour(3, 0, 0)

    def send_b(da, dz, s):
        send_whole(s, rel(da, dz, 3), b_up)
        send_whole(s, rel(da, dz, 1), b_down)

    def send_z(da, s):
        send_whole(s, rel(da, 3, 0), z_up)
        send_whole(s, rel(da, 1, 0), z_down)

    def place(s):
        mid = lax.rem(lax.div(s + 4, 8), 2)
        q = (1 - mid) * lax.rem(s, 4) + mid * lax.div(lax.rem(s + 4, 8), 2)
        dz = mid * (1 + 2 * lax.rem(s, 2)) + (1 - mid) * 2 * lax.div(s, 12)
        da = q + lax.div(q, 2) * (5 - 2 * q)
        return q, da, dz

    def plane(s):
        q, da, dz = place(s)
        p, r = slot(da, dz, 0), rel(da, dz, 0)

        @pl.when(s == 1)
        def _():
            wait_half(p, r, 0)
            wait_half(p, r, 1)
            send_half(p, 0, irel(2, 0, 0), a_down)

        @pl.when(s == 2)
        def _():
            wait_half(p, r, 0)
            wait_half(p, r, 1)
            send_half(p, 1, irel(2, 0, 0), a_up)

        @pl.when(s == 3)
        def _():
            wait_half(p, r, 0)
            wait_half(p, r, 1)

        @pl.when(s < 4)
        def _():
            send_z(da, p)

        @pl.when(jnp.logical_and(s >= 4, s < 12))
        def _():
            wait_piece(p, r, q == 0)

            @pl.when(dz == 1)
            def _():
                send_half(p, 0, rel(da, 2, 0), z_down)

            @pl.when(dz == 3)
            def _():
                send_half(p, 1, rel(da, 2, 0), z_up)

        @pl.when(s >= 12)
        def _():
            wait_half(p, r, 0)
            wait_half(p, r, 1)

        send_b(da, dz, p)
        send_sib(p, r)

    def cross1(s):
        _, da, dz = place(s)
        for db, k, dev in ((1, 0, b_down), (3, 1, b_up)):
            p, r = slot(da, dz, db), rel(da, dz, db)
            wait_piece(p, r, s == 0)
            send_half(p, k, rel(da, dz, 2), dev)
            send_sib(p, r)

    def cross2(s):
        _, da, dz = place(s)
        p, r = slot(da, dz, 2), rel(da, dz, 2)
        wait_half(p, r, 0)
        wait_half(p, r, 1)
        send_sib(p, r)

    def multiply(h, da, dz, pa, pb_is_row):
        pz = lax.rem(z + dz, 4)
        first = pz * 16 + pa * 4
        total = None
        for i in range(4):
            lhs = jnp.concatenate([buf[h, first + i, 0], buf[h, first + i, 1]], axis=1)
            j = pz * 16 + (1 - h) * (i * 4 + pa) + h * (pa * 4 + i)
            part = lax.dot_general(lhs, w[j], NT, preferred_element_type=F32)
            total = part if total is None else total + part
        acc[h] += total

    def multiply_own(s):
        _, da, dz = place(s)

        @pl.when(s == 0)
        def _():
            local[0].wait()

        multiply(c, da, dz, lax.rem(a + da, 4), None)

    def multiply_sib(s):
        _, da, dz = place(s)
        pa = lax.rem(b + da, 4)
        pz = lax.rem(z + dz, 4)

        def wait_sib(db):
            t = pz * 16 + pa * 4 + lax.rem(a + db, 4)
            remote(buf.at[o, t], buf.at[o, t], sib_ssem, sib_rsem.at[rel(da, dz, db)], sibling).wait_recv()

        @pl.when(s == 0)
        def _():
            local[1].wait()
            remote(own_rows(o), buf.at[o, me_other, o], sib_ssem, own_rsem.at[0], sibling).wait_recv()

        @pl.when(s > 0)
        def _():
            wait_sib(0)

        for db in (1, 3, 2):
            wait_sib(db)
        multiply(o, da, dz, pa, None)

    def dequantize(ch):
        code_load(ch).wait()

        @pl.loop(0, 4)
        def _(i):
            for g in range(2):
                rows = pl.ds(g * 128, 128)
                word = cbuf[ch, rows, pl.ds(pl.multiple_of(i * 256, 256), 256)]
                j = ch * 4 + i
                for part, level in ((0, word), (1, lax.shift_right_logical(word, 4))):
                    col = pl.ds(pl.multiple_of((j + 32 * part) * 256, 256), 256)
                    level = jnp.bitwise_and(level, 15)
                    value = sc_v[g : g + 1, col] * (level - ze_v[g : g + 1, col]).astype(F32)
                    w[j + 32 * part, rows, :] = value.astype(BF16)

    def along_x(d):
        return chip(lax.rem(x + d, 4), y, z, c)

    def along_y(d):
        return chip(x, lax.rem(y + d, 4), z, c)

    def along_z(d):
        return chip(x, y, lax.rem(z + d, 4), c)

    def all_to_all(src, dst, base, way):
        return [small(src(d), dst, base + d - 1, way(d)) for d in (1, 2, 3)]

    def scatter_x():
        return all_to_all(lambda d: r0.at[lax.rem(x + d, 4)], s1.at[x], 1, along_x)

    def sum_z():
        return all_to_all(lambda d: s2.at[z], s2.at[z], 4, along_z)

    def sum_y():
        return all_to_all(lambda d: s3.at[y], s3.at[y], 7, along_y)

    def gather_x():
        return all_to_all(lambda d: s4.at[x], s4.at[x], 10, along_x)

    def share():
        return small(fin.at[c], fin.at[c], 13, sibling)

    def swap():
        return small(ad_mine, ad_peer, 14, partner)

    def begin(copies):
        for copy in copies:
            copy.start()

    def end(copies):
        for copy in copies:
            copy.wait_recv()

    def four(ref):
        return ((ref[0] + ref[1]) + ref[2]) + ref[3]

    def stage1():
        small(p_src.at[o], p_dst, 0, sibling).wait_recv()
        for i in range(4):
            rows = pl.ds(i * 8, 8)
            r0[i] = p_src[c, rows, :] + p_dst[rows, :]
        s1[x] = r0[x]
        begin(scatter_x())

    def stage2():
        end(scatter_x())
        s2[z] = four(s1)
        begin(sum_z())

    def stage3():
        end(sum_z())
        s3[y] = four(s2)
        begin(sum_y())

    def stage4():
        end(sum_y())
        s4[x] = four(s3)
        begin(gather_x())

    def stage5():
        end(gather_x())
        for i in range(4):
            fin[c, pl.ds(i * 8, 8), :] = s4[i]
        share().start()

    def stage6():
        share().wait_recv()
        ain = None
        aout = None
        for h in range(2):
            rows = pl.ds(h * 256, 256)
            left = fin[h, 0:16, :].astype(BF16)
            right = fin[h, 16:32, :].astype(BF16)
            acc[h] += SCALE * lax.dot_general(right, am_v[...], TN, preferred_element_type=F32)
            p1 = jnp.dot(right, hid[rows, :], preferred_element_type=F32)
            p2 = jnp.dot(left, og_v[rows, :], preferred_element_type=F32)
            ain = p1 if ain is None else ain + p1
            aout = p2 if aout is None else aout + p2
        ad_mine[:, 0:256] = (SCALE / tokens) * ain
        ad_mine[:, 256:384] = (SCALE / tokens) * aout
        swap().start()

    def stage7():
        swap().wait_recv()
        ad_sum[...] = ad_mine[...] + ad_peer[...]
        for copy in adapter_out:
            copy.start()

    adapter_out = [
        pltpu.make_async_copy(ad_sum.at[:, 0:256], ain_out, out_sem.at[4]),
        pltpu.make_async_copy(ad_sum.at[:, 256:384], aout_out, out_sem.at[5]),
    ]

    loads[5].wait()
    loads[6].wait()

    @pl.loop(1, STEPS + LAG_SIB)
    def _(s):
        for at, stage in ((1, stage1), (2, stage2), (4, stage3), (6, stage4), (8, stage5), (10, stage6), (13, stage7)):
            pl.when(s == at)(stage)

        @pl.when(s < STEPS)
        def _():
            plane(s)

        @pl.when(jnp.logical_and(s >= LAG1, s < STEPS + LAG1))
        def _():
            cross1(s - LAG1)

        @pl.when(jnp.logical_and(s >= LAG2, s < STEPS + LAG2))
        def _():
            cross2(s - LAG2)

        @pl.when(s <= 4)
        def _():
            dequantize(s * 2 - 2)
            dequantize(s * 2 - 1)

        @pl.when(jnp.logical_and(s >= LAG_OWN, s < STEPS + LAG_OWN))
        def _():
            multiply_own(s - LAG_OWN)

        @pl.when(s >= LAG_SIB)
        def _():
            multiply_sib(s - LAG_SIB)

    outs = []
    for h in range(2):
        rows = pl.ds(h * 256, 256)
        gh = acc[h]
        gres[rows, :] = (gh * f2[rows, :]).astype(BF16)
        ures[rows, :] = (gh * f1[rows, :]).astype(BF16)
        for i, (v, ref) in enumerate(((gres, gate_out), (ures, up_out))):
            copy = pltpu.make_async_copy(v.at[rows], ref.at[rows], out_sem.at[h * 2 + i])
            copy.start()
            outs.append(copy)

    small(p_src.at[o], p_dst, 0, sibling).wait_send()
    for copies in (scatter_x(), sum_z(), sum_y(), gather_x(), [share()], [swap()]):
        for copy in copies:
            copy.wait_send()
    remote(buf.at[0, 0:63], buf.at[0, 0:63], ssem, rsem.at[0], sibling).wait_send()
    remote(buf.at[0], buf.at[0], sib_ssem, rsem.at[0], sibling).wait_send()
    for copy in outs + adapter_out:
        copy.wait()


def local(og, gate, up, codes, scales, zeros, amap, omap):
    rows, cols = og.shape
    hidden = gate.shape[1]
    tokens = rows * lax.axis_size("dp")
    anywhere = pl.BlockSpec(memory_space=pl.ANY)
    dma = pltpu.SemaphoreType.DMA
    return pl.pallas_call(
        functools.partial(kernel, tokens),
        out_shape=(
            jax.ShapeDtypeStruct((rows, hidden), BF16),
            jax.ShapeDtypeStruct((rows, hidden), BF16),
            jax.ShapeDtypeStruct((16, hidden), F32),
            jax.ShapeDtypeStruct((16, cols), F32),
        ),
        in_specs=[anywhere] * 8,
        out_specs=[anywhere] * 4,
        scratch_shapes=[
            pltpu.VMEM((2, 64, 2, 256, 128), BF16),
            pltpu.VMEM((64, 256, 256), BF16),
            pltpu.VMEM((8, 256, 1024), jnp.int32),
            pltpu.VMEM((2, 16384), F32),
            pltpu.VMEM((2, 16384), jnp.int32),
            pltpu.VMEM((512, 256), BF16),
            pltpu.VMEM((512, 256), BF16),
            pltpu.VMEM((16, 256), BF16),
            pltpu.VMEM((16, 128), BF16),
            pltpu.VMEM((512, 128), BF16),
            pltpu.VMEM((512, 256), BF16),
            pltpu.VMEM((512, 256), F32),
            pltpu.VMEM((512, 256), F32),
            pltpu.VMEM((2, 256, 256), F32),
            pltpu.VMEM((512, 256), BF16),
            pltpu.VMEM((512, 256), BF16),
            pltpu.VMEM((2, 32, 256), F32),
            pltpu.VMEM((32, 256), F32),
            pltpu.VMEM((4, 8, 256), F32),
            pltpu.VMEM((4, 8, 256), F32),
            pltpu.VMEM((4, 8, 256), F32),
            pltpu.VMEM((4, 8, 256), F32),
            pltpu.VMEM((4, 8, 256), F32),
            pltpu.VMEM((2, 32, 256), F32),
            pltpu.VMEM((16, 384), F32),
            pltpu.VMEM((16, 384), F32),
            pltpu.VMEM((16, 384), F32),
            dma((7,)),
            dma((8,)),
            dma((2,)),
            dma,
            dma,
            dma((128,)),
            dma((64,)),
            dma((2,)),
            dma((15,)),
            dma((15,)),
            dma((6,)),
        ],
        compiler_params=pltpu.CompilerParams(
            collective_id=0, has_side_effects=True, vmem_limit_bytes=58 * 2**20
        ),
        name="backward",
    )(og, gate, up, codes, scales, zeros, amap, omap)


def solution(mesh):
    in_specs = (
        P("dp", "fsdp"),
        P("dp", "fsdp"),
        P("dp", "fsdp"),
        P("fsdp", None),
        P("fsdp", None),
        P("fsdp", None),
        P(None, "fsdp"),
        P(None, "fsdp"),
    )
    out_specs = (P("dp", "fsdp"), P("dp", "fsdp"), P(None, "fsdp"), P(None, "fsdp"))
    return jax.shard_map(local, mesh=mesh, in_specs=in_specs, out_specs=out_specs, check_vma=False)
```

```python
import functools

import jax
import jax.numpy as jnp
from jax import lax
from jax.experimental import pallas as pl
from jax.experimental.pallas import tpu as pltpu
from jax.sharding import PartitionSpec as P

MESH = pl.DeviceIdType.MESH
F32 = jnp.float32
BF16 = jnp.bfloat16
SCALE = 2.0
LAG1, LAG2, LAG_OWN, LAG_SIB = 3, 6, 7, 8
STEPS = 16
ORDER = ((0, 0), (1, 0), (3, 0), (0, 1), (0, 3), (2, 0), (0, 2), (1, 1), (1, 3), (1, 2), (3, 2), (3, 1), (3, 3), (2, 2), (2, 1), (2, 3))
Z_SENDS = ((2, 1), (6, 3), (8, 2))
Z_HALVES = 2
CROSS_FIRST = (3, 7)
EARLY = 6
STAGES = ((2, 2), (5, 3), (7, 4), (9, 5), (11, 6), (14, 7))
NT = (((1,), (1,)), ((), ()))
TN = (((0,), (0,)), ((), ()))


def kernel(
    tokens,
    og, gate, up, codes, scales, zeros, amap, omap,
    gate_out, up_out, ain_out, aout_out,
    buf, w, cbuf, sc_v, ze_v, gate_v, up_v, am_v, om_v, og_v,
    hid, f1, f2, acc,
    p_src, p_dst, r0, s1, s2, s3, s4, fin, ad_mine, ad_peer,
    load_sem, code_sem, local_sem, ssem, sib_ssem, plane_sem, half_sem, near_sem, far_sem, sib_rsem, own_rsem,
    small_ssem, small_rsem,
):
    dp = lax.axis_index("dp")
    f = lax.axis_index("fsdp")
    c = lax.rem(f, 2)
    y = lax.rem(lax.div(f, 2), 4)
    x = lax.rem(lax.div(f, 8), 4)
    z = lax.div(f, 32)
    a = y + c * (x - y)
    b = x + c * (y - x)
    o = 1 - c

    def chip(px, py, pz, core):
        return (dp, ((pz * 4 + px) * 4 + py) * 2 + core)

    def neighbour(da, dz, db):
        pa, pz, pb = lax.rem(a + da, 4), lax.rem(z + dz, 4), lax.rem(b + db, 4)
        return chip(pb + c * (pa - pb), pa + c * (pb - pa), pz, c)

    sibling = (dp, f + 1 - 2 * c)
    partner = (1 - dp, f)

    def slot(da, dz, db):
        return lax.rem(z + dz, 4) * 16 + lax.rem(a + da, 4) * 4 + lax.rem(b + db, 4)

    def pair(da, dz):
        return lax.rem(dz, 4) * 4 + lax.rem(da, 4)

    me = slot(0, 0, 0)
    me_other = z * 16 + b * 4 + a

    bar = pltpu.get_barrier_semaphore()
    peers = [neighbour(1, 0, 0), neighbour(2, 0, 0), neighbour(3, 0, 0)]
    peers += [neighbour(0, 1, 0), neighbour(0, 2, 0), neighbour(0, 3, 0)]
    peers += [neighbour(0, 0, 1), neighbour(0, 0, 2), neighbour(0, 0, 3)]
    peers += [sibling, partner]
    for peer in peers:
        pl.semaphore_signal(bar, inc=1, device_id=peer, device_id_type=MESH)

    sems = (0, 0, 0, 1, 2, 3, 3)
    pairs = ((og, og_v), (gate, gate_v), (up, up_v), (amap, am_v), (omap, om_v), (scales, sc_v), (zeros, ze_v))
    loads = [pltpu.make_async_copy(p[0], p[1], load_sem.at[i]) for i, p in zip(sems, pairs)]
    for load in loads:
        load.start()

    def code_load(ch):
        return pltpu.make_async_copy(
            codes.at[:, pl.ds(pl.multiple_of(ch * 1024, 1024), 1024)], cbuf.at[ch], code_sem.at[ch // 4]
        )

    for ch in range(8):
        code_load(ch).start()

    def remote(src, dst, s_sem, r_sem, dev):
        return pltpu.make_async_remote_copy(
            src_ref=src, dst_ref=dst, send_sem=s_sem, recv_sem=r_sem, device_id=dev, device_id_type=MESH
        )

    def small(src, dst, i, dev):
        return remote(src, dst, small_ssem, small_rsem.at[i], dev)

    def own_rows(h):
        return og.at[pl.ds(pl.multiple_of(h * 256, 256), 256)]

    a_up, a_down = neighbour(1, 0, 0), neighbour(3, 0, 0)
    b_up, b_down = neighbour(0, 0, 1), neighbour(0, 0, 3)
    z_up, z_down = neighbour(0, 1, 0), neighbour(0, 3, 0)

    def send_own(src, k):
        for i, dev in ((3, z_up), (2, z_down), (1, a_up), (0, a_down)):
            remote(src, buf.at[c, me, k], ssem, half_sem.at[i * 2 + k], dev).start()

    pl.semaphore_wait(bar, len(peers))

    def wait_slots(n, sem):
        remote(buf.at[c, 0:n], buf.at[c, 0:n], ssem, sem, sibling).wait_recv()

    def wait_half(i, k):
        remote(buf.at[c, 0, k], buf.at[c, 0, k], ssem, half_sem.at[i * 2 + k], sibling).wait_recv()

    def send_whole(s, sem, dev):
        remote(buf.at[c, s], buf.at[c, s], ssem, sem, dev).start()

    def send_half(s, k, sem, dev):
        remote(buf.at[c, s, k], buf.at[c, s, k], ssem, sem, dev).start()

    def send_sib(s, da, dz):
        remote(buf.at[c, s], buf.at[c, s], sib_ssem, sib_rsem.at[pair(da, dz)], sibling).start()

    def send_b(da, dz, s):
        send_whole(s, near_sem.at[pair(da, dz)], b_up)
        send_whole(s, near_sem.at[pair(da, dz)], b_down)

    def send_z(da, s):
        send_whole(s, plane_sem.at[pair(da, 3)], z_up)
        send_whole(s, plane_sem.at[pair(da, 1)], z_down)

    def send_a(dz, s):
        send_whole(s, plane_sem.at[pair(3, dz)], a_up)
        send_whole(s, plane_sem.at[pair(1, dz)], a_down)

    sib_own_c = remote(own_rows(c), buf.at[c, me, c], sib_ssem, own_rsem.at[0], sibling)
    sib_own_o = remote(own_rows(o), buf.at[o, me_other, c], sib_ssem, own_rsem.at[1], sibling)
    sib_own_o.start()
    send_own(own_rows(c), c)
    local = [
        pltpu.make_async_copy(own_rows(c), buf.at[c, me, c], local_sem.at[0]),
        pltpu.make_async_copy(own_rows(o), buf.at[o, me_other, c], local_sem.at[1]),
    ]
    for copy in local:
        copy.start()
    sib_own_c.start()

    def partial_sums(h):
        rows = pl.ds(pl.multiple_of(h * 256, 256), 256)
        g = gate_v[rows, :].astype(F32)
        u = up_v[rows, :].astype(F32)
        sig = 1.0 / (1.0 + jnp.exp(-g))
        silu = g * sig
        hid[rows, :] = (silu * u).astype(BF16)
        f1[rows, :] = silu
        f2[rows, :] = u * sig * (1.0 + g * (1.0 - sig))
        p_src[h, 0:16, :] = lax.dot_general(am_v[...], hid[rows, :], NT, preferred_element_type=F32)
        p_src[h, 16:32, :] = lax.dot_general(om_v[...], og_v[rows, :], NT, preferred_element_type=F32)

    pltpu.make_async_copy(w.at[0:5], w.at[0:5], load_sem.at[0]).wait()
    loads[3].wait()
    loads[4].wait()
    partial_sums(o)
    small(p_src.at[o], p_dst, 0, sibling).start()
    remote(own_rows(o), buf.at[c, me, o], sib_ssem, own_rsem.at[1], sibling).wait_recv()
    send_own(buf.at[c, me, o], o)
    local[0].wait()
    send_b(0, 0, me)

    def place(s):
        da = sum(jnp.where(s == i, v[0], 0) for i, v in enumerate(ORDER) if v[0])
        dz = sum(jnp.where(s == i, v[1], 0) for i, v in enumerate(ORDER) if v[1])
        return da, dz

    def plane(s):
        da, dz = place(s)
        p = slot(da, dz, 0)
        along_a = lax.rem(dz, 2) == 0
        one, three = da == 1, da == 3
        own_a = jnp.logical_and(lax.rem(da, 2) == 1, dz == 0)
        own_z = jnp.logical_and(da == 0, lax.rem(dz, 2) == 1)

        @pl.when(jnp.logical_not(jnp.logical_or(own_a, own_z)))
        def _():
            wait_slots(1, plane_sem.at[pair(da, dz)])

        @pl.when(own_a)
        def _():
            pl.when(one)(lambda: wait_half(0, 0))
            pl.when(three)(lambda: wait_half(1, 1))

        @pl.when(along_a)
        def _():
            pl.when(one)(lambda: send_half(p, 0, plane_sem.at[pair(2, dz)], a_down))
            pl.when(three)(lambda: send_half(p, 1, plane_sem.at[pair(2, dz)], a_up))

        @pl.when(own_a)
        def _():
            pl.when(one)(lambda: wait_half(0, 1))
            pl.when(three)(lambda: wait_half(1, 0))

        @pl.when(own_z)
        def _():
            pl.when(dz == 1)(lambda: wait_half(2, 1))
            pl.when(dz == 3)(lambda: wait_half(3, 0))

        @pl.when(jnp.logical_and(da == 0, dz == 2))
        def _():
            send_a(dz, p)

        send_b(da, dz, p)
        send_sib(p, da, dz)

    def z_sends(s):
        @pl.when(s == Z_HALVES)
        def _():
            wait_half(2, 0)
            send_half(slot(0, 1, 0), 0, plane_sem.at[pair(0, 2)], z_down)
            wait_half(3, 1)
            send_half(slot(0, 3, 0), 1, plane_sem.at[pair(0, 2)], z_up)

        for at, which in Z_SENDS:

            @pl.when(s == at)
            def _(which=which):
                send_z(which, slot(which, 0, 0))

    def cross1(s):
        da, dz = place(s)
        wait_slots(2, near_sem.at[pair(da, dz)])
        for db, k, dev in ((1, 0, b_down), (3, 1, b_up)):
            p = slot(da, dz, db)
            send_half(p, k, far_sem.at[pair(da, dz)], dev)
            send_sib(p, da, dz)

    def cross2(s):
        da, dz = place(s)
        wait_slots(1, far_sem.at[pair(da, dz)])
        send_sib(slot(da, dz, 2), da, dz)

    def multiply(h, dz, pa):
        pz = lax.rem(z + dz, 4)
        first = pz * 16 + pa * 4
        total = None
        for i in range(4):
            lhs = jnp.concatenate([buf[h, first + i, 0], buf[h, first + i, 1]], axis=1)
            j = pz * 16 + (1 - h) * (i * 4 + pa) + h * (pa * 4 + i)
            part = lax.dot_general(lhs, w[j], NT, preferred_element_type=F32)
            total = part if total is None else total + part
        acc[h] += total

    def multiply_own(s):
        da, dz = place(s)

        multiply(c, dz, lax.rem(a + da, 4))

    def multiply_sib(s):
        da, dz = place(s)
        pa = lax.rem(b + da, 4)

        def wait_sib(n):
            slots = buf.at[o, 0:n]
            remote(slots, slots, sib_ssem, sib_rsem.at[pair(da, dz)], sibling).wait_recv()

        @pl.when(s == 0)
        def _():
            local[1].wait()
            remote(own_rows(o), buf.at[o, me_other, o], sib_ssem, own_rsem.at[0], sibling).wait_recv()
            wait_sib(3)

        @pl.when(s > 0)
        def _():
            wait_sib(4)

        multiply(o, dz, pa)

    def dequantize(ch):
        @pl.when(ch % 4 == 0)
        def _():
            pltpu.make_async_copy(cbuf.at[0:4], cbuf.at[0:4], code_sem.at[ch // 4]).wait()

        @pl.loop(0, 4)
        def _(i):
            for g in range(2):
                rows = pl.ds(g * 128, 128)
                word = cbuf[ch, rows, pl.ds(pl.multiple_of(i * 256, 256), 256)]
                j = ch * 4 + i
                for part, level in ((0, word), (1, lax.shift_right_logical(word, 4))):
                    col = pl.ds(pl.multiple_of((j + 32 * part) * 256, 256), 256)
                    level = jnp.bitwise_and(level, 15)
                    value = sc_v[g : g + 1, col] * (level - ze_v[g : g + 1, col]).astype(F32)
                    w[j + 32 * part, rows, :] = value.astype(BF16)

    def along_x(d):
        return chip(lax.rem(x + d, 4), y, z, c)

    def along_y(d):
        return chip(x, lax.rem(y + d, 4), z, c)

    def along_z(d):
        return chip(x, y, lax.rem(z + d, 4), c)

    def all_to_all(src, dst, base, way):
        return [small(src(d), dst, base, way(d)) for d in (1, 2, 3)]

    def scatter_x():
        return all_to_all(lambda d: r0.at[lax.rem(x + d, 4)], s1.at[x], 1, along_x)

    def sum_z():
        return all_to_all(lambda d: s2.at[z], s2.at[z], 2, along_z)

    def sum_y():
        return all_to_all(lambda d: s3.at[y], s3.at[y], 3, along_y)

    def gather_x():
        return all_to_all(lambda d: s4.at[x], s4.at[x], 4, along_x)

    def share():
        return small(fin.at[c], fin.at[c], 5, sibling)

    def swap():
        return small(ad_mine, ad_peer, 6, partner)

    def begin(copies):
        for copy in copies:
            copy.start()

    def end(ref, i):
        small(ref.at[0:3], ref.at[0:3], i, sibling).wait_recv()

    def four(ref):
        return ((ref[0] + ref[1]) + ref[2]) + ref[3]

    def stage1():
        small(p_src.at[o], p_dst, 0, sibling).wait_recv()
        for i in range(4):
            rows = pl.ds(i * 8, 8)
            r0[i] = p_src[c, rows, :] + p_dst[rows, :]
        s1[x] = r0[x]
        begin(scatter_x())

    def stage2():
        end(s1, 1)
        s2[z] = four(s1)
        begin(sum_z())

    def stage3():
        end(s2, 2)
        s3[y] = four(s2)
        begin(sum_y())

    def stage4():
        end(s3, 3)
        s4[x] = four(s3)
        begin(gather_x())

    def stage5():
        end(s4, 4)
        for i in range(4):
            fin[c, pl.ds(i * 8, 8), :] = s4[i]
        share().start()

    def stage6():
        share().wait_recv()
        ain = None
        aout = None
        for h in range(2):
            rows = pl.ds(h * 256, 256)
            left = fin[h, 0:16, :].astype(BF16)
            right = fin[h, 16:32, :].astype(BF16)
            acc[h] += SCALE * lax.dot_general(right, am_v[...], TN, preferred_element_type=F32)
            p1 = jnp.dot(right, hid[rows, :], preferred_element_type=F32)
            p2 = jnp.dot(left, og_v[rows, :], preferred_element_type=F32)
            ain = p1 if ain is None else ain + p1
            aout = p2 if aout is None else aout + p2
        ad_mine[:, 0:256] = (SCALE / tokens) * ain
        ad_mine[:, 256:384] = (SCALE / tokens) * aout
        swap().start()

    def stage7():
        swap().wait_recv()
        ain_out[...] = ad_mine[:, 0:256] + ad_peer[:, 0:256]
        aout_out[...] = ad_mine[:, 256:384] + ad_peer[:, 256:384]

    partial_sums(c)
    stage1()
    acc[...] = jnp.zeros_like(acc)
    pltpu.make_async_copy(w.at[0:2], w.at[0:2], load_sem.at[3]).wait()
    for ch in range(EARLY):
        dequantize(ch)

    @pl.loop(1, STEPS + LAG_SIB)
    def _(s):
        for at, stage in STAGES:
            pl.when(s == at)((stage2, stage3, stage4, stage5, stage6, stage7)[stage - 2])

        early = jnp.logical_and(s >= CROSS_FIRST[0], s < CROSS_FIRST[1])

        @pl.when(jnp.logical_and(s < STEPS, jnp.logical_not(early)))
        def _():
            plane(s)

        z_sends(s)

        @pl.when(jnp.logical_and(s >= LAG1, s < STEPS + LAG1))
        def _():
            cross1(s - LAG1)

        @pl.when(early)
        def _():
            plane(s)

        @pl.when(s <= 8 - EARLY)
        def _():
            dequantize(s + EARLY - 1)

        @pl.when(jnp.logical_and(s >= LAG_OWN, s < STEPS + LAG_OWN))
        def _():
            multiply_own(s - LAG_OWN)

        @pl.when(s >= LAG_SIB)
        def _():
            multiply_sib(s - LAG_SIB)

        @pl.when(jnp.logical_and(s >= LAG2, s < STEPS + LAG2))
        def _():
            cross2(s - LAG2)

    for h in range(2):
        rows = pl.ds(h * 256, 256)
        gh = acc[h]
        gate_out[rows, :] = (gh * f2[rows, :]).astype(BF16)
        up_out[rows, :] = (gh * f1[rows, :]).astype(BF16)

    remote(f1.at[0:184], f1.at[0:184], small_ssem, own_rsem.at[0], sibling).wait_send()
    remote(buf.at[0, 0:63], buf.at[0, 0:63], ssem, own_rsem.at[0], sibling).wait_send()
    remote(buf.at[0], buf.at[0], sib_ssem, own_rsem.at[0], sibling).wait_send()


def local(og, gate, up, codes, scales, zeros, amap, omap):
    rows, cols = og.shape
    hidden = gate.shape[1]
    tokens = rows * lax.axis_size("dp")
    anywhere = pl.BlockSpec(memory_space=pl.ANY)
    dma = pltpu.SemaphoreType.DMA
    shapes = (
        jax.ShapeDtypeStruct((rows, hidden), BF16),
        jax.ShapeDtypeStruct((rows, hidden), BF16),
        jax.ShapeDtypeStruct((16, hidden), F32),
        jax.ShapeDtypeStruct((16, cols), F32),
    )
    return pl.pallas_call(
        functools.partial(kernel, tokens),
        out_shape=tuple(pltpu.VMEM(v.shape, v.dtype) for v in shapes),
        in_specs=[anywhere] * 8,
        out_specs=[pl.BlockSpec(memory_space=pltpu.VMEM)] * 4,
        scratch_shapes=[
            pltpu.VMEM((2, 64, 2, 256, 128), BF16),
            pltpu.VMEM((64, 256, 256), BF16),
            pltpu.VMEM((8, 256, 1024), jnp.int32),
            pltpu.VMEM((2, 16384), F32),
            pltpu.VMEM((2, 16384), jnp.int32),
            pltpu.VMEM((512, 256), BF16),
            pltpu.VMEM((512, 256), BF16),
            pltpu.VMEM((16, 256), BF16),
            pltpu.VMEM((16, 128), BF16),
            pltpu.VMEM((512, 128), BF16),
            pltpu.VMEM((512, 256), BF16),
            pltpu.VMEM((512, 256), F32),
            pltpu.VMEM((512, 256), F32),
            pltpu.VMEM((2, 256, 256), F32),
            pltpu.VMEM((2, 32, 256), F32),
            pltpu.VMEM((32, 256), F32),
            pltpu.VMEM((4, 8, 256), F32),
            pltpu.VMEM((4, 8, 256), F32),
            pltpu.VMEM((4, 8, 256), F32),
            pltpu.VMEM((4, 8, 256), F32),
            pltpu.VMEM((4, 8, 256), F32),
            pltpu.VMEM((2, 32, 256), F32),
            pltpu.VMEM((16, 384), F32),
            pltpu.VMEM((16, 384), F32),
            dma((4,)),
            dma((2,)),
            dma((2,)),
            dma,
            dma,
            dma((16,)),
            dma((8,)),
            dma((16,)),
            dma((16,)),
            dma((16,)),
            dma((2,)),
            dma,
            dma((7,)),
        ],
        compiler_params=pltpu.CompilerParams(
            collective_id=0, has_side_effects=True, vmem_limit_bytes=58 * 2**20
        ),
        name="backward",
    )(og, gate, up, codes, scales, zeros, amap, omap)


def solution(mesh):
    in_specs = (
        P("dp", "fsdp"),
        P("dp", "fsdp"),
        P("dp", "fsdp"),
        P("fsdp", None),
        P("fsdp", None),
        P("fsdp", None),
        P(None, "fsdp"),
        P(None, "fsdp"),
    )
    out_specs = (P("dp", "fsdp"), P("dp", "fsdp"), P(None, "fsdp"), P(None, "fsdp"))
    return jax.shard_map(local, mesh=mesh, in_specs=in_specs, out_specs=out_specs, check_vma=False)
```

```python
import functools

import jax
import jax.numpy as jnp
from jax import lax
from jax.experimental import pallas as pl
from jax.experimental.pallas import tpu as pltpu
from jax.sharding import PartitionSpec as P

MESH = pl.DeviceIdType.MESH
F32 = jnp.float32
BF16 = jnp.bfloat16
SCALE = 2.0
LAG1, LAG2, LAG_OWN, LAG_SIB = 3, 6, 7, 8
STEPS = 16
ORDER = ((0, 0), (1, 0), (3, 0), (0, 1), (0, 3), (2, 0), (0, 2), (1, 1), (1, 3), (1, 2), (3, 2), (3, 1), (3, 3), (2, 2), (2, 1), (2, 3))
Z_SENDS = ((3, 1), (6, 3), (8, 2))
Z_HALVES = (2, 3)
CROSS_FIRST = (3, 7)
EARLY = 6
STAGES = ((4, 1), (6, 2), (9, 3), (11, 4), (13, 5), (14, 6), (17, 7))
NT = (((1,), (1,)), ((), ()))
TN = (((0,), (0,)), ((), ()))


def kernel(
    tokens,
    og, gate, up, codes, scales, zeros, amap, omap,
    gate_out, up_out, ain_out, aout_out,
    buf, w, cbuf, sc_v, ze_v, gate_v, up_v, am_v, om_v, og_v,
    hid, f1, f2, acc,
    p_src, p_dst, r0, s1, s2, s3, s4, fin, ad_mine, ad_peer,
    load_sem, code_sem, local_sem, ssem, sib_ssem, plane_sem, half_sem, near_sem, far_sem, sib_rsem, own_rsem,
    small_ssem, small_rsem,
):
    dp = lax.axis_index("dp")
    f = lax.axis_index("fsdp")
    c = lax.rem(f, 2)
    y = lax.rem(lax.div(f, 2), 4)
    x = lax.rem(lax.div(f, 8), 4)
    z = lax.div(f, 32)
    a = y + c * (x - y)
    b = x + c * (y - x)
    o = 1 - c

    def chip(px, py, pz, core):
        return (dp, ((pz * 4 + px) * 4 + py) * 2 + core)

    def neighbour(da, dz, db, core=None):
        pa, pz, pb = lax.rem(a + da, 4), lax.rem(z + dz, 4), lax.rem(b + db, 4)
        return chip(pb + c * (pa - pb), pa + c * (pb - pa), pz, c if core is None else core)

    sibling = (dp, f + 1 - 2 * c)
    partner = (1 - dp, f)

    def slot(da, dz, db):
        return lax.rem(z + dz, 4) * 16 + lax.rem(a + da, 4) * 4 + lax.rem(b + db, 4)

    def pair(da, dz):
        return lax.rem(dz, 4) * 4 + lax.rem(da, 4)

    me = slot(0, 0, 0)
    me_other = z * 16 + b * 4 + a

    bar = pltpu.get_barrier_semaphore()
    peers = [neighbour(1, 0, 0), neighbour(3, 0, 0)]
    peers += [neighbour(0, 1, 0), neighbour(0, 3, 0)]
    peers += [neighbour(0, 0, 1), neighbour(0, 0, 3)]
    peers += [neighbour(1, 0, 0, o), neighbour(3, 0, 0, o)]
    peers += [sibling, partner]
    for peer in peers:
        pl.semaphore_signal(bar, inc=1, device_id=peer, device_id_type=MESH)

    sems = (0, 0, 0, 1, 2, 3, 3)
    pairs = ((og, og_v), (gate, gate_v), (up, up_v), (amap, am_v), (omap, om_v), (scales, sc_v), (zeros, ze_v))
    loads = [pltpu.make_async_copy(p[0], p[1], load_sem.at[i]) for i, p in zip(sems, pairs)]
    for load in loads:
        load.start()

    def code_load(ch):
        return pltpu.make_async_copy(
            codes.at[:, pl.ds(pl.multiple_of(ch * 1024, 1024), 1024)], cbuf.at[ch], code_sem.at[ch // 4]
        )

    for ch in range(8):
        code_load(ch).start()

    def remote(src, dst, s_sem, r_sem, dev):
        return pltpu.make_async_remote_copy(
            src_ref=src, dst_ref=dst, send_sem=s_sem, recv_sem=r_sem, device_id=dev, device_id_type=MESH
        )

    def small(src, dst, i, dev):
        return remote(src, dst, small_ssem, small_rsem.at[i], dev)

    def own_rows(h):
        return og.at[pl.ds(pl.multiple_of(h * 256, 256), 256)]

    a_up, a_down = neighbour(1, 0, 0), neighbour(3, 0, 0)
    b_up, b_down = neighbour(0, 0, 1), neighbour(0, 0, 3)
    z_up, z_down = neighbour(0, 1, 0), neighbour(0, 3, 0)

    def send_own_z(src, k):
        for i, dev in ((3, z_up), (2, z_down)):
            remote(src, buf.at[c, me, k], ssem, half_sem.at[i * 2 + k], dev).start()

    pl.semaphore_wait(bar, len(peers))

    def wait_slots(n, sem):
        remote(buf.at[c, 0:n], buf.at[c, 0:n], ssem, sem, sibling).wait_recv()

    def wait_half(i, k):
        remote(buf.at[c, 0, k], buf.at[c, 0, k], ssem, half_sem.at[i * 2 + k], sibling).wait_recv()

    def send_whole(s, sem, dev):
        remote(buf.at[c, s], buf.at[c, s], ssem, sem, dev).start()

    def send_half(s, k, sem, dev):
        remote(buf.at[c, s, k], buf.at[c, s, k], ssem, sem, dev).start()

    def send_sib(s, da, dz):
        remote(buf.at[c, s], buf.at[c, s], sib_ssem, sib_rsem.at[pair(da, dz)], sibling).start()

    def send_b(da, dz, s):
        send_whole(s, near_sem.at[pair(da, dz)], b_up)
        send_whole(s, near_sem.at[pair(da, dz)], b_down)

    def send_z(da, s):
        send_whole(s, plane_sem.at[pair(da, 3)], z_up)
        send_whole(s, plane_sem.at[pair(da, 1)], z_down)

    def send_a(dz, s):
        send_whole(s, plane_sem.at[pair(3, dz)], a_up)
        send_whole(s, plane_sem.at[pair(1, dz)], a_down)

    sib_own_c = remote(own_rows(c), buf.at[c, me, c], sib_ssem, own_rsem.at[0], sibling)
    sib_own_o = remote(own_rows(o), buf.at[o, me_other, c], sib_ssem, own_rsem.at[1], sibling)
    sib_own_o.start()
    send_own_z(own_rows(c), c)
    for i, h, place_of, dev in (
        (1, c, me, a_up),
        (0, c, me, a_down),
        (1, o, me_other, neighbour(0, 0, 1, o)),
        (0, o, me_other, neighbour(0, 0, 3, o)),
    ):
        remote(own_rows(h), buf.at[h, place_of, c], ssem, half_sem.at[i * 2 + c], dev).start()
    local = [
        pltpu.make_async_copy(own_rows(c), buf.at[c, me, c], local_sem.at[0]),
        pltpu.make_async_copy(own_rows(o), buf.at[o, me_other, c], local_sem.at[1]),
    ]
    for copy in local:
        copy.start()
    sib_own_c.start()

    def partial_sums(h):
        rows = pl.ds(pl.multiple_of(h * 256, 256), 256)
        g = gate_v[rows, :].astype(F32)
        u = up_v[rows, :].astype(F32)
        sig = 1.0 / (1.0 + jnp.exp(-g))
        silu = g * sig
        hid[rows, :] = (silu * u).astype(BF16)
        f1[rows, :] = silu
        f2[rows, :] = u * sig * (1.0 + g * (1.0 - sig))
        p_src[h, 0:16, :] = lax.dot_general(am_v[...], hid[rows, :], NT, preferred_element_type=F32)
        p_src[h, 16:32, :] = lax.dot_general(om_v[...], og_v[rows, :], NT, preferred_element_type=F32)

    pltpu.make_async_copy(w.at[0:5], w.at[0:5], load_sem.at[0]).wait()
    loads[3].wait()
    loads[4].wait()
    partial_sums(o)
    small(p_src.at[o], p_dst, 0, sibling).start()
    remote(own_rows(o), buf.at[c, me, o], sib_ssem, own_rsem.at[1], sibling).wait_recv()
    send_own_z(buf.at[c, me, o], o)
    local[0].wait()
    send_b(0, 0, me)

    def place(s):
        da = sum(jnp.where(s == i, v[0], 0) for i, v in enumerate(ORDER) if v[0])
        dz = sum(jnp.where(s == i, v[1], 0) for i, v in enumerate(ORDER) if v[1])
        return da, dz

    def plane(s):
        da, dz = place(s)
        p = slot(da, dz, 0)
        along_a = lax.rem(dz, 2) == 0
        one, three = da == 1, da == 3
        own_a = jnp.logical_and(lax.rem(da, 2) == 1, dz == 0)
        own_z = jnp.logical_and(da == 0, lax.rem(dz, 2) == 1)

        @pl.when(jnp.logical_not(jnp.logical_or(own_a, own_z)))
        def _():
            wait_slots(1, plane_sem.at[pair(da, dz)])

        @pl.when(own_a)
        def _():
            pl.when(one)(lambda: wait_half(0, 0))
            pl.when(three)(lambda: wait_half(1, 1))

        @pl.when(along_a)
        def _():
            pl.when(one)(lambda: send_half(p, 0, plane_sem.at[pair(2, dz)], a_down))
            pl.when(three)(lambda: send_half(p, 1, plane_sem.at[pair(2, dz)], a_up))

        @pl.when(own_a)
        def _():
            pl.when(one)(lambda: wait_half(0, 1))
            pl.when(three)(lambda: wait_half(1, 0))

        @pl.when(own_z)
        def _():
            pl.when(dz == 1)(lambda: wait_half(2, o))
            pl.when(dz == 3)(lambda: wait_half(3, c))

        @pl.when(jnp.logical_and(da == 0, dz == 2))
        def _():
            send_a(dz, p)

        send_b(da, dz, p)
        send_sib(p, da, dz)

    def z_sends(s):
        @pl.when(s == Z_HALVES[0])
        def _():
            wait_half(2, c)
            send_half(slot(0, 1, 0), c, plane_sem.at[pair(0, 2)], z_down)

        @pl.when(s == Z_HALVES[1])
        def _():
            wait_half(3, o)
            send_half(slot(0, 3, 0), o, plane_sem.at[pair(0, 2)], z_up)

        for at, which in Z_SENDS:

            @pl.when(s == at)
            def _(which=which):
                send_z(which, slot(which, 0, 0))

    def cross1(s):
        da, dz = place(s)
        wait_slots(2, near_sem.at[pair(da, dz)])
        for db, k, dev in ((1, 0, b_down), (3, 1, b_up)):
            p = slot(da, dz, db)
            send_half(p, k, far_sem.at[pair(da, dz)], dev)
            send_sib(p, da, dz)

    def cross2(s):
        da, dz = place(s)
        wait_slots(1, far_sem.at[pair(da, dz)])
        send_sib(slot(da, dz, 2), da, dz)

    def multiply(h, dz, pa):
        pz = lax.rem(z + dz, 4)
        first = pz * 16 + pa * 4
        total = None
        for i in range(4):
            lhs = jnp.concatenate([buf[h, first + i, 0], buf[h, first + i, 1]], axis=1)
            j = pz * 16 + (1 - h) * (i * 4 + pa) + h * (pa * 4 + i)
            part = lax.dot_general(lhs, w[j], NT, preferred_element_type=F32)
            total = part if total is None else total + part
        acc[h] += total

    def multiply_own(s):
        da, dz = place(s)

        multiply(c, dz, lax.rem(a + da, 4))

    def multiply_sib(s):
        da, dz = place(s)
        pa = lax.rem(b + da, 4)

        def wait_sib(n):
            slots = buf.at[o, 0:n]
            remote(slots, slots, sib_ssem, sib_rsem.at[pair(da, dz)], sibling).wait_recv()

        @pl.when(s == 0)
        def _():
            local[1].wait()
            remote(own_rows(o), buf.at[o, me_other, o], sib_ssem, own_rsem.at[0], sibling).wait_recv()
            wait_sib(3)

        @pl.when(s > 0)
        def _():
            wait_sib(4)

        multiply(o, dz, pa)

    def dequantize(ch):
        @pl.when(ch % 4 == 0)
        def _():
            pltpu.make_async_copy(cbuf.at[0:4], cbuf.at[0:4], code_sem.at[ch // 4]).wait()

        @pl.loop(0, 4)
        def _(i):
            for g in range(2):
                rows = pl.ds(g * 128, 128)
                word = cbuf[ch, rows, pl.ds(pl.multiple_of(i * 256, 256), 256)]
                j = ch * 4 + i
                for part, level in ((0, word), (1, lax.shift_right_logical(word, 4))):
                    col = pl.ds(pl.multiple_of((j + 32 * part) * 256, 256), 256)
                    level = jnp.bitwise_and(level, 15)
                    value = sc_v[g : g + 1, col] * (level - ze_v[g : g + 1, col]).astype(F32)
                    w[j + 32 * part, rows, :] = value.astype(BF16)

    def along_x(d):
        return chip(lax.rem(x + d, 4), y, z, c)

    def along_y(d):
        return chip(x, lax.rem(y + d, 4), z, c)

    def along_z(d):
        return chip(x, y, lax.rem(z + d, 4), c)

    def all_to_all(src, dst, base, way):
        return [small(src(d), dst, base, way(d)) for d in (1, 2, 3)]

    def scatter_x():
        return all_to_all(lambda d: r0.at[lax.rem(x + d, 4)], s1.at[x], 1, along_x)

    def sum_z():
        return all_to_all(lambda d: s2.at[z], s2.at[z], 2, along_z)

    def sum_y():
        return all_to_all(lambda d: s3.at[y], s3.at[y], 3, along_y)

    def gather_x():
        return all_to_all(lambda d: s4.at[x], s4.at[x], 4, along_x)

    def share():
        return small(fin.at[c], fin.at[c], 5, sibling)

    def swap():
        return small(ad_mine, ad_peer, 6, partner)

    def begin(copies):
        for copy in copies:
            copy.start()

    def end(ref, i):
        small(ref.at[0:3], ref.at[0:3], i, sibling).wait_recv()

    def four(ref):
        return ((ref[0] + ref[1]) + ref[2]) + ref[3]

    def stage1():
        small(p_src.at[o], p_dst, 0, sibling).wait_recv()
        for i in range(4):
            rows = pl.ds(i * 8, 8)
            r0[i] = p_src[c, rows, :] + p_dst[rows, :]
        s1[x] = r0[x]
        begin(scatter_x())

    def stage2():
        end(s1, 1)
        s2[z] = four(s1)
        begin(sum_z())

    def stage3():
        end(s2, 2)
        s3[y] = four(s2)
        begin(sum_y())

    def stage4():
        end(s3, 3)
        s4[x] = four(s3)
        begin(gather_x())

    def stage5():
        end(s4, 4)
        for i in range(4):
            fin[c, pl.ds(i * 8, 8), :] = s4[i]
        share().start()

    def stage6():
        share().wait_recv()
        ain = None
        aout = None
        for h in range(2):
            rows = pl.ds(h * 256, 256)
            left = fin[h, 0:16, :].astype(BF16)
            right = fin[h, 16:32, :].astype(BF16)
            acc[h] += SCALE * lax.dot_general(right, am_v[...], TN, preferred_element_type=F32)
            p1 = jnp.dot(right, hid[rows, :], preferred_element_type=F32)
            p2 = jnp.dot(left, og_v[rows, :], preferred_element_type=F32)
            ain = p1 if ain is None else ain + p1
            aout = p2 if aout is None else aout + p2
        ad_mine[:, 0:256] = (SCALE / tokens) * ain
        ad_mine[:, 256:384] = (SCALE / tokens) * aout
        swap().start()

    def stage7():
        swap().wait_recv()
        ain_out[...] = ad_mine[:, 0:256] + ad_peer[:, 0:256]
        aout_out[...] = ad_mine[:, 256:384] + ad_peer[:, 256:384]

    partial_sums(c)
    acc[...] = jnp.zeros_like(acc)
    pltpu.make_async_copy(w.at[0:2], w.at[0:2], load_sem.at[3]).wait()
    for ch in range(EARLY):
        dequantize(ch)

    stages = (stage1, stage2, stage3, stage4, stage5, stage6, stage7)

    @pl.loop(1, STEPS + LAG_SIB)
    def _(s):
        for at, stage in STAGES:
            pl.when(s == at)(stages[stage - 1])

        early = jnp.logical_and(s >= CROSS_FIRST[0], s < CROSS_FIRST[1])

        @pl.when(jnp.logical_and(s < STEPS, jnp.logical_not(early)))
        def _():
            plane(s)

        @pl.when(jnp.logical_and(s >= LAG1, s < STEPS + LAG1))
        def _():
            cross1(s - LAG1)

        z_sends(s)

        @pl.when(early)
        def _():
            plane(s)

        @pl.when(s <= 8 - EARLY)
        def _():
            dequantize(s + EARLY - 1)

        @pl.when(s >= LAG_SIB)
        def _():
            multiply_sib(s - LAG_SIB)

        @pl.when(jnp.logical_and(s >= LAG2, s < STEPS + LAG2))
        def _():
            cross2(s - LAG2)

        @pl.when(jnp.logical_and(s >= LAG_OWN, s < STEPS + LAG_OWN))
        def _():
            multiply_own(s - LAG_OWN)

    for h in range(2):
        rows = pl.ds(h * 256, 256)
        gh = acc[h]
        gate_out[rows, :] = (gh * f2[rows, :]).astype(BF16)
        up_out[rows, :] = (gh * f1[rows, :]).astype(BF16)

    remote(f1.at[0:184], f1.at[0:184], small_ssem, own_rsem.at[0], sibling).wait_send()
    remote(buf.at[0, 0:63], buf.at[0, 0:63], ssem, own_rsem.at[0], sibling).wait_send()
    remote(buf.at[0], buf.at[0], sib_ssem, own_rsem.at[0], sibling).wait_send()


def hand_over(*refs):
    n = len(refs) // 2
    copies = [pltpu.make_async_copy(refs[i], refs[n + i], refs[-1].at[i]) for i in range(n)]
    for copy in copies:
        copy.start()
    for copy in copies:
        copy.wait()


def local(og, gate, up, codes, scales, zeros, amap, omap):
    rows, cols = og.shape
    hidden = gate.shape[1]
    tokens = rows * lax.axis_size("dp")
    anywhere = pl.BlockSpec(memory_space=pl.ANY)
    dma = pltpu.SemaphoreType.DMA
    shapes = (
        jax.ShapeDtypeStruct((rows, hidden), BF16),
        jax.ShapeDtypeStruct((rows, hidden), BF16),
        jax.ShapeDtypeStruct((16, hidden), F32),
        jax.ShapeDtypeStruct((16, cols), F32),
    )
    results = pl.pallas_call(
        functools.partial(kernel, tokens),
        out_shape=tuple(pltpu.VMEM(v.shape, v.dtype) for v in shapes),
        in_specs=[anywhere] * 8,
        out_specs=[pl.BlockSpec(memory_space=pltpu.VMEM)] * 4,
        scratch_shapes=[
            pltpu.VMEM((2, 64, 2, 256, 128), BF16),
            pltpu.VMEM((64, 256, 256), BF16),
            pltpu.VMEM((8, 256, 1024), jnp.int32),
            pltpu.VMEM((2, 16384), F32),
            pltpu.VMEM((2, 16384), jnp.int32),
            pltpu.VMEM((512, 256), BF16),
            pltpu.VMEM((512, 256), BF16),
            pltpu.VMEM((16, 256), BF16),
            pltpu.VMEM((16, 128), BF16),
            pltpu.VMEM((512, 128), BF16),
            pltpu.VMEM((512, 256), BF16),
            pltpu.VMEM((512, 256), F32),
            pltpu.VMEM((512, 256), F32),
            pltpu.VMEM((2, 256, 256), F32),
            pltpu.VMEM((2, 32, 256), F32),
            pltpu.VMEM((32, 256), F32),
            pltpu.VMEM((4, 8, 256), F32),
            pltpu.VMEM((4, 8, 256), F32),
            pltpu.VMEM((4, 8, 256), F32),
            pltpu.VMEM((4, 8, 256), F32),
            pltpu.VMEM((4, 8, 256), F32),
            pltpu.VMEM((2, 32, 256), F32),
            pltpu.VMEM((16, 384), F32),
            pltpu.VMEM((16, 384), F32),
            dma((4,)),
            dma((2,)),
            dma((2,)),
            dma,
            dma,
            dma((16,)),
            dma((8,)),
            dma((16,)),
            dma((16,)),
            dma((16,)),
            dma((2,)),
            dma,
            dma((7,)),
        ],
        compiler_params=pltpu.CompilerParams(
            collective_id=0, has_side_effects=True, vmem_limit_bytes=58 * 2**20
        ),
        name="backward",
    )(og, gate, up, codes, scales, zeros, amap, omap)
    return pl.pallas_call(
        hand_over,
        out_shape=shapes,
        in_specs=[pl.BlockSpec(memory_space=pltpu.VMEM)] * 4,
        out_specs=[anywhere] * 4,
        scratch_shapes=[dma((4,))],
        name="hand_over",
    )(*(pltpu.with_memory_space_constraint(v, pltpu.VMEM) for v in results))


def solution(mesh):
    in_specs = (
        P("dp", "fsdp"),
        P("dp", "fsdp"),
        P("dp", "fsdp"),
        P("fsdp", None),
        P("fsdp", None),
        P("fsdp", None),
        P(None, "fsdp"),
        P(None, "fsdp"),
    )
    out_specs = (P("dp", "fsdp"), P("dp", "fsdp"), P(None, "fsdp"), P(None, "fsdp"))
    return jax.shard_map(local, mesh=mesh, in_specs=in_specs, out_specs=out_specs, check_vma=False)
```

```python
import functools

import jax
import jax.numpy as jnp
from jax import lax
from jax.experimental import pallas as pl
from jax.experimental.pallas import tpu as pltpu
from jax.sharding import PartitionSpec as P

MESH = pl.DeviceIdType.MESH
F32 = jnp.float32
BF16 = jnp.bfloat16
SCALE = 2.0
LAG1, LAG2, LAG_OWN, LAG_SIB = 3, 6, 7, 8
STEPS = 16
ORDER = ((0, 0), (1, 0), (3, 0), (0, 1), (0, 3), (2, 0), (0, 2), (1, 1), (1, 3), (1, 2), (3, 2), (3, 1), (3, 3), (2, 2), (2, 1), (2, 3))
Z_SENDS = ((3, 1), (8, 3), (10, 2))
Z_HALVES = (2, 3)
Z_FAR = 12
SOONER = (13, 14)
CROSS_FIRST = (3, 9)
EARLY = 6
STAGES = ((4, 1), (7, 2), (10, 3), (12, 4), (14, 5), (16, 6), (18, 7))
NT = (((1,), (1,)), ((), ()))
TN = (((0,), (0,)), ((), ()))


def kernel(
    tokens,
    og, gate, up, codes, scales, zeros, amap, omap,
    gate_out, up_out, ain_out, aout_out,
    buf, w, cbuf, sc_v, ze_v, gate_v, up_v, am_v, om_v, og_v,
    hid, f1, f2, acc,
    p_src, p_dst, r0, s1, s2, s3, s4, fin, ad_mine, ad_peer,
    load_sem, code_sem, local_sem, ssem, sib_ssem, plane_sem, half_sem, near_sem, far_sem, sib_rsem, own_rsem,
    small_ssem, small_rsem,
):
    dp = lax.axis_index("dp")
    f = lax.axis_index("fsdp")
    c = lax.rem(f, 2)
    y = lax.rem(lax.div(f, 2), 4)
    x = lax.rem(lax.div(f, 8), 4)
    z = lax.div(f, 32)
    a = y + c * (x - y)
    b = x + c * (y - x)
    o = 1 - c

    def chip(px, py, pz, core):
        return (dp, ((pz * 4 + px) * 4 + py) * 2 + core)

    def neighbour(da, dz, db, core=None):
        pa, pz, pb = lax.rem(a + da, 4), lax.rem(z + dz, 4), lax.rem(b + db, 4)
        return chip(pb + c * (pa - pb), pa + c * (pb - pa), pz, c if core is None else core)

    sibling = (dp, f + 1 - 2 * c)
    partner = (1 - dp, f)

    def slot(da, dz, db):
        return lax.rem(z + dz, 4) * 16 + lax.rem(a + da, 4) * 4 + lax.rem(b + db, 4)

    def pair(da, dz):
        return lax.rem(dz, 4) * 4 + lax.rem(da, 4)

    me = slot(0, 0, 0)
    me_other = z * 16 + b * 4 + a

    bar = pltpu.get_barrier_semaphore()
    peers = [neighbour(1, 0, 0), neighbour(3, 0, 0)]
    peers += [neighbour(0, 1, 0), neighbour(0, 3, 0)]
    peers += [neighbour(0, 0, 1), neighbour(0, 0, 3)]
    peers += [neighbour(1, 0, 0, o), neighbour(3, 0, 0, o)]
    peers += [sibling, partner]
    for peer in peers:
        pl.semaphore_signal(bar, inc=1, device_id=peer, device_id_type=MESH)

    sems = (0, 0, 0, 1, 2, 3, 3)
    pairs = ((og, og_v), (gate, gate_v), (up, up_v), (amap, am_v), (omap, om_v), (scales, sc_v), (zeros, ze_v))
    loads = [pltpu.make_async_copy(p[0], p[1], load_sem.at[i]) for i, p in zip(sems, pairs)]
    for load in loads:
        load.start()

    def code_load(ch):
        return pltpu.make_async_copy(
            codes.at[:, pl.ds(pl.multiple_of(ch * 1024, 1024), 1024)], cbuf.at[ch], code_sem.at[ch // 4]
        )

    for ch in range(8):
        code_load(ch).start()

    def remote(src, dst, s_sem, r_sem, dev):
        return pltpu.make_async_remote_copy(
            src_ref=src, dst_ref=dst, send_sem=s_sem, recv_sem=r_sem, device_id=dev, device_id_type=MESH
        )

    def small(src, dst, i, dev):
        return remote(src, dst, small_ssem, small_rsem.at[i], dev)

    def own_rows(h):
        return og.at[pl.ds(pl.multiple_of(h * 256, 256), 256)]

    a_up, a_down = neighbour(1, 0, 0), neighbour(3, 0, 0)
    b_up, b_down = neighbour(0, 0, 1), neighbour(0, 0, 3)
    z_up, z_down = neighbour(0, 1, 0), neighbour(0, 3, 0)

    def send_own_z(src, k):
        for i, dev in ((3, z_up), (2, z_down)):
            remote(src, buf.at[c, me, k], ssem, half_sem.at[i * 2 + k], dev).start()

    pl.semaphore_wait(bar, len(peers))

    def wait_slots(n, sem):
        remote(buf.at[c, 0:n], buf.at[c, 0:n], ssem, sem, sibling).wait_recv()

    def wait_half(i, k):
        remote(buf.at[c, 0, k], buf.at[c, 0, k], ssem, half_sem.at[i * 2 + k], sibling).wait_recv()

    def send_whole(s, sem, dev):
        remote(buf.at[c, s], buf.at[c, s], ssem, sem, dev).start()

    def send_half(s, k, sem, dev):
        remote(buf.at[c, s, k], buf.at[c, s, k], ssem, sem, dev).start()

    def send_sib(s, da, dz):
        remote(buf.at[c, s], buf.at[c, s], sib_ssem, sib_rsem.at[pair(da, dz)], sibling).start()

    def send_b(da, dz, s):
        send_whole(s, near_sem.at[pair(da, dz)], b_up)
        send_whole(s, near_sem.at[pair(da, dz)], b_down)

    def send_z(da, s):
        send_whole(s, plane_sem.at[pair(da, 3)], z_up)
        send_whole(s, plane_sem.at[pair(da, 1)], z_down)

    def send_a(dz, s):
        send_whole(s, plane_sem.at[pair(3, dz)], a_up)
        send_whole(s, plane_sem.at[pair(1, dz)], a_down)

    sib_own_c = remote(own_rows(c), buf.at[c, me, c], sib_ssem, own_rsem.at[0], sibling)
    sib_own_o = remote(own_rows(o), buf.at[o, me_other, c], sib_ssem, own_rsem.at[1], sibling)
    sib_own_o.start()
    send_own_z(own_rows(c), c)
    for i, h, place_of, dev in (
        (1, c, me, a_up),
        (0, c, me, a_down),
        (1, o, me_other, neighbour(0, 0, 1, o)),
        (0, o, me_other, neighbour(0, 0, 3, o)),
    ):
        remote(own_rows(h), buf.at[h, place_of, c], ssem, half_sem.at[i * 2 + c], dev).start()
    local = [
        pltpu.make_async_copy(own_rows(c), buf.at[c, me, c], local_sem.at[0]),
        pltpu.make_async_copy(own_rows(o), buf.at[o, me_other, c], local_sem.at[1]),
    ]
    for copy in local:
        copy.start()
    sib_own_c.start()

    def partial_sums(h):
        rows = pl.ds(pl.multiple_of(h * 256, 256), 256)
        g = gate_v[rows, :].astype(F32)
        u = up_v[rows, :].astype(F32)
        sig = 1.0 / (1.0 + jnp.exp(-g))
        silu = g * sig
        hid[rows, :] = (silu * u).astype(BF16)
        f1[rows, :] = silu
        f2[rows, :] = u * sig * (1.0 + g * (1.0 - sig))
        p_src[h, 0:16, :] = lax.dot_general(am_v[...], hid[rows, :], NT, preferred_element_type=F32)
        p_src[h, 16:32, :] = lax.dot_general(om_v[...], og_v[rows, :], NT, preferred_element_type=F32)

    pltpu.make_async_copy(w.at[0:5], w.at[0:5], load_sem.at[0]).wait()
    loads[3].wait()
    loads[4].wait()
    partial_sums(o)
    small(p_src.at[o], p_dst, 0, sibling).start()
    remote(own_rows(o), buf.at[c, me, o], sib_ssem, own_rsem.at[1], sibling).wait_recv()
    send_own_z(buf.at[c, me, o], o)
    local[0].wait()
    send_b(0, 0, me)

    def place(s):
        da = sum(jnp.where(s == i, v[0], 0) for i, v in enumerate(ORDER) if v[0])
        dz = sum(jnp.where(s == i, v[1], 0) for i, v in enumerate(ORDER) if v[1])
        return da, dz

    def plane(s):
        da, dz = place(s)
        p = slot(da, dz, 0)
        along_a = lax.rem(dz, 2) == 0
        one, three = da == 1, da == 3
        own_a = jnp.logical_and(lax.rem(da, 2) == 1, dz == 0)
        own_z = jnp.logical_and(da == 0, lax.rem(dz, 2) == 1)

        @pl.when(jnp.logical_not(jnp.logical_or(own_a, own_z)))
        def _():
            wait_slots(1, plane_sem.at[pair(da, dz)])

        @pl.when(own_a)
        def _():
            pl.when(one)(lambda: wait_half(0, 0))
            pl.when(three)(lambda: wait_half(1, 1))

        @pl.when(along_a)
        def _():
            pl.when(one)(lambda: send_half(p, 0, plane_sem.at[pair(2, dz)], a_down))
            pl.when(three)(lambda: send_half(p, 1, plane_sem.at[pair(2, dz)], a_up))

        @pl.when(own_a)
        def _():
            pl.when(one)(lambda: wait_half(0, 1))
            pl.when(three)(lambda: wait_half(1, 0))

        @pl.when(own_z)
        def _():
            pl.when(dz == 1)(lambda: wait_half(2, o))
            pl.when(dz == 3)(lambda: wait_half(3, c))

        @pl.when(jnp.logical_and(da == 0, dz == 2))
        def _():
            send_a(dz, p)

        send_b(da, dz, p)
        send_sib(p, da, dz)

    def z_sends(s):
        @pl.when(s == Z_HALVES[0])
        def _():
            wait_half(2, c)
            send_half(slot(0, 1, 0), c, plane_sem.at[pair(0, 2)], z_down)

        @pl.when(s == Z_HALVES[1])
        def _():
            wait_half(3, o)
            send_half(slot(0, 3, 0), o, plane_sem.at[pair(0, 2)], z_up)

        for at, which in Z_SENDS:

            @pl.when(s == at)
            def _(which=which):
                send_z(which, slot(which, 0, 0))

        @pl.when(s == Z_FAR)
        def _():
            p = slot(2, 0, 2)
            send_whole(p, far_sem.at[pair(2, 3)], z_up)
            send_whole(p, far_sem.at[pair(2, 1)], z_down)

    def cross1(s):
        da, dz = place(s)
        wait_slots(2, near_sem.at[pair(da, dz)])
        along_b = jnp.logical_not(jnp.logical_and(da == 2, lax.rem(dz, 2) == 1))
        for db, k, dev in ((1, 0, b_down), (3, 1, b_up)):
            p = slot(da, dz, db)

            @pl.when(along_b)
            def _(p=p, k=k, dev=dev):
                send_half(p, k, far_sem.at[pair(da, dz)], dev)

            send_sib(p, da, dz)

    def cross2(s):
        da, dz = place(s)
        wait_slots(1, far_sem.at[pair(da, dz)])
        send_sib(slot(da, dz, 2), da, dz)

    def multiply(h, dz, pa):
        pz = lax.rem(z + dz, 4)
        first = pz * 16 + pa * 4
        total = None
        for i in range(4):
            lhs = jnp.concatenate([buf[h, first + i, 0], buf[h, first + i, 1]], axis=1)
            j = pz * 16 + (1 - h) * (i * 4 + pa) + h * (pa * 4 + i)
            part = lax.dot_general(lhs, w[j], NT, preferred_element_type=F32)
            total = part if total is None else total + part
        acc[h] += total

    def multiply_own(s):
        da, dz = place(s)

        multiply(c, dz, lax.rem(a + da, 4))

    def multiply_sib(s):
        da, dz = place(s)
        pa = lax.rem(b + da, 4)

        def wait_sib(n):
            slots = buf.at[o, 0:n]
            remote(slots, slots, sib_ssem, sib_rsem.at[pair(da, dz)], sibling).wait_recv()

        @pl.when(s == 0)
        def _():
            local[1].wait()
            remote(own_rows(o), buf.at[o, me_other, o], sib_ssem, own_rsem.at[0], sibling).wait_recv()
            wait_sib(3)

        @pl.when(s > 0)
        def _():
            wait_sib(4)

        multiply(o, dz, pa)

    def dequantize(ch):
        @pl.when(ch % 4 == 0)
        def _():
            pltpu.make_async_copy(cbuf.at[0:4], cbuf.at[0:4], code_sem.at[ch // 4]).wait()

        @pl.loop(0, 4)
        def _(i):
            for g in range(2):
                rows = pl.ds(g * 128, 128)
                word = cbuf[ch, rows, pl.ds(pl.multiple_of(i * 256, 256), 256)]
                j = ch * 4 + i
                for part, level in ((0, word), (1, lax.shift_right_logical(word, 4))):
                    col = pl.ds(pl.multiple_of((j + 32 * part) * 256, 256), 256)
                    level = jnp.bitwise_and(level, 15)
                    value = sc_v[g : g + 1, col] * (level - ze_v[g : g + 1, col]).astype(F32)
                    w[j + 32 * part, rows, :] = value.astype(BF16)

    def along_x(d):
        return chip(lax.rem(x + d, 4), y, z, c)

    def along_y(d):
        return chip(x, lax.rem(y + d, 4), z, c)

    def along_z(d):
        return chip(x, y, lax.rem(z + d, 4), c)

    def all_to_all(src, dst, base, way):
        return [small(src(d), dst, base, way(d)) for d in (1, 2, 3)]

    def scatter_x():
        return all_to_all(lambda d: r0.at[lax.rem(x + d, 4)], s1.at[x], 1, along_x)

    def sum_z():
        return all_to_all(lambda d: s2.at[z], s2.at[z], 2, along_z)

    def sum_y():
        return all_to_all(lambda d: s3.at[y], s3.at[y], 3, along_y)

    def gather_x():
        return all_to_all(lambda d: s4.at[x], s4.at[x], 4, along_x)

    def share():
        return small(fin.at[c], fin.at[c], 5, sibling)

    def swap():
        return small(ad_mine, ad_peer, 6, partner)

    def begin(copies):
        for copy in copies:
            copy.start()

    def end(ref, i):
        small(ref.at[0:3], ref.at[0:3], i, sibling).wait_recv()

    def four(ref):
        return ((ref[0] + ref[1]) + ref[2]) + ref[3]

    def stage1():
        small(p_src.at[o], p_dst, 0, sibling).wait_recv()
        for i in range(4):
            rows = pl.ds(i * 8, 8)
            r0[i] = p_src[c, rows, :] + p_dst[rows, :]
        s1[x] = r0[x]
        begin(scatter_x())

    def stage2():
        end(s1, 1)
        s2[z] = four(s1)
        begin(sum_z())

    def stage3():
        end(s2, 2)
        s3[y] = four(s2)
        begin(sum_y())

    def stage4():
        end(s3, 3)
        s4[x] = four(s3)
        begin(gather_x())

    def stage5():
        end(s4, 4)
        for i in range(4):
            fin[c, pl.ds(i * 8, 8), :] = s4[i]
        share().start()

    def stage6():
        share().wait_recv()
        ain = None
        aout = None
        for h in range(2):
            rows = pl.ds(h * 256, 256)
            left = fin[h, 0:16, :].astype(BF16)
            right = fin[h, 16:32, :].astype(BF16)
            acc[h] += SCALE * lax.dot_general(right, am_v[...], TN, preferred_element_type=F32)
            p1 = jnp.dot(right, hid[rows, :], preferred_element_type=F32)
            p2 = jnp.dot(left, og_v[rows, :], preferred_element_type=F32)
            ain = p1 if ain is None else ain + p1
            aout = p2 if aout is None else aout + p2
        ad_mine[:, 0:256] = (SCALE / tokens) * ain
        ad_mine[:, 256:384] = (SCALE / tokens) * aout
        swap().start()

    def stage7():
        swap().wait_recv()
        ain_out[...] = ad_mine[:, 0:256] + ad_peer[:, 0:256]
        aout_out[...] = ad_mine[:, 256:384] + ad_peer[:, 256:384]

    partial_sums(c)
    acc[...] = jnp.zeros_like(acc)
    pltpu.make_async_copy(w.at[0:2], w.at[0:2], load_sem.at[3]).wait()
    for ch in range(EARLY):
        dequantize(ch)

    stages = (stage1, stage2, stage3, stage4, stage5, stage6, stage7)

    def catch_up(do, s, lag, sooner):
        late = jnp.where(s < sooner, s - lag, s - lag + 1)
        lax.fori_loop(jnp.maximum(jnp.where(s <= sooner, s - lag, late), 0), late + 1, lambda i, _: do(i), None)

    @pl.loop(1, STEPS + LAG1)
    def _(s):
        for at, stage in STAGES:
            pl.when(s == at)(stages[stage - 1])

        early = jnp.logical_and(s >= CROSS_FIRST[0], s < CROSS_FIRST[1])

        @pl.when(jnp.logical_and(s < STEPS, jnp.logical_not(early)))
        def _():
            plane(s)

        @pl.when(jnp.logical_and(s >= LAG1, s < STEPS + LAG1))
        def _():
            cross1(s - LAG1)

        z_sends(s)

        @pl.when(early)
        def _():
            plane(s)

        @pl.when(s <= 8 - EARLY)
        def _():
            dequantize(s + EARLY - 1)

        catch_up(multiply_sib, s, LAG_SIB, SOONER[1])

        @pl.when(s >= LAG2)
        def _():
            cross2(s - LAG2)

        catch_up(multiply_own, s, LAG_OWN, SOONER[0])

    @pl.loop(STEPS + LAG1 - LAG2, STEPS)
    def _(s):
        cross2(s)

    @pl.loop(STEPS + LAG1 - LAG2, STEPS)
    def _(s):
        multiply_own(s)
        multiply_sib(s - 1)

    multiply_sib(STEPS - 1)

    for h in range(2):
        rows = pl.ds(h * 256, 256)
        gh = acc[h]
        gate_out[rows, :] = (gh * f2[rows, :]).astype(BF16)
        up_out[rows, :] = (gh * f1[rows, :]).astype(BF16)

    remote(f1.at[0:184], f1.at[0:184], small_ssem, own_rsem.at[0], sibling).wait_send()
    remote(buf.at[0, 0:63], buf.at[0, 0:63], ssem, own_rsem.at[0], sibling).wait_send()
    remote(buf.at[0], buf.at[0], sib_ssem, own_rsem.at[0], sibling).wait_send()


def hand_over(*refs):
    n = len(refs) // 2
    copies = [pltpu.make_async_copy(refs[i], refs[n + i], refs[-1].at[i]) for i in range(n)]
    for copy in copies:
        copy.start()
    for copy in copies:
        copy.wait()


def local(og, gate, up, codes, scales, zeros, amap, omap):
    rows, cols = og.shape
    hidden = gate.shape[1]
    tokens = rows * lax.axis_size("dp")
    anywhere = pl.BlockSpec(memory_space=pl.ANY)
    dma = pltpu.SemaphoreType.DMA
    shapes = (
        jax.ShapeDtypeStruct((rows, hidden), BF16),
        jax.ShapeDtypeStruct((rows, hidden), BF16),
        jax.ShapeDtypeStruct((16, hidden), F32),
        jax.ShapeDtypeStruct((16, cols), F32),
    )
    results = pl.pallas_call(
        functools.partial(kernel, tokens),
        out_shape=tuple(pltpu.VMEM(v.shape, v.dtype) for v in shapes),
        in_specs=[anywhere] * 8,
        out_specs=[pl.BlockSpec(memory_space=pltpu.VMEM)] * 4,
        scratch_shapes=[
            pltpu.VMEM((2, 64, 2, 256, 128), BF16),
            pltpu.VMEM((64, 256, 256), BF16),
            pltpu.VMEM((8, 256, 1024), jnp.int32),
            pltpu.VMEM((2, 16384), F32),
            pltpu.VMEM((2, 16384), jnp.int32),
            pltpu.VMEM((512, 256), BF16),
            pltpu.VMEM((512, 256), BF16),
            pltpu.VMEM((16, 256), BF16),
            pltpu.VMEM((16, 128), BF16),
            pltpu.VMEM((512, 128), BF16),
            pltpu.VMEM((512, 256), BF16),
            pltpu.VMEM((512, 256), F32),
            pltpu.VMEM((512, 256), F32),
            pltpu.VMEM((2, 256, 256), F32),
            pltpu.VMEM((2, 32, 256), F32),
            pltpu.VMEM((32, 256), F32),
            pltpu.VMEM((4, 8, 256), F32),
            pltpu.VMEM((4, 8, 256), F32),
            pltpu.VMEM((4, 8, 256), F32),
            pltpu.VMEM((4, 8, 256), F32),
            pltpu.VMEM((4, 8, 256), F32),
            pltpu.VMEM((2, 32, 256), F32),
            pltpu.VMEM((16, 384), F32),
            pltpu.VMEM((16, 384), F32),
            dma((4,)),
            dma((2,)),
            dma((2,)),
            dma,
            dma,
            dma((16,)),
            dma((8,)),
            dma((16,)),
            dma((16,)),
            dma((16,)),
            dma((2,)),
            dma,
            dma((7,)),
        ],
        compiler_params=pltpu.CompilerParams(
            collective_id=0, has_side_effects=True, vmem_limit_bytes=58 * 2**20
        ),
        name="backward",
    )(og, gate, up, codes, scales, zeros, amap, omap)
    return pl.pallas_call(
        hand_over,
        out_shape=shapes,
        in_specs=[pl.BlockSpec(memory_space=pltpu.VMEM)] * 4,
        out_specs=[anywhere] * 4,
        scratch_shapes=[dma((4,))],
        name="hand_over",
    )(*(pltpu.with_memory_space_constraint(v, pltpu.VMEM) for v in results))


def solution(mesh):
    in_specs = (
        P("dp", "fsdp"),
        P("dp", "fsdp"),
        P("dp", "fsdp"),
        P("fsdp", None),
        P("fsdp", None),
        P("fsdp", None),
        P(None, "fsdp"),
        P(None, "fsdp"),
    )
    out_specs = (P("dp", "fsdp"), P("dp", "fsdp"), P(None, "fsdp"), P(None, "fsdp"))
    return jax.shard_map(local, mesh=mesh, in_specs=in_specs, out_specs=out_specs, check_vma=False)
```

```python
import functools

import jax
import jax.numpy as jnp
from jax import lax
from jax.experimental import pallas as pl
from jax.experimental.pallas import tpu as pltpu
from jax.sharding import PartitionSpec as P

MESH = pl.DeviceIdType.MESH
F32 = jnp.float32
BF16 = jnp.bfloat16
SCALE = 2.0
LAG1, LAG2, LAG_OWN, LAG_SIB = 3, 6, 7, 8
STEPS = 16
ORDER = ((0, 0), (1, 0), (3, 0), (0, 1), (0, 3), (2, 0), (0, 2), (1, 1), (1, 3), (1, 2), (3, 2), (3, 1), (3, 3), (2, 2), (2, 1), (2, 3))
Z_SENDS = ((3, 1), (8, 3), (10, 2))
Z_HALVES = (2, 3)
Z_FAR = ((12, 2),)
SOONER = (13, 17)
CROSS_FIRST = (3, 9)
EARLY = 6
STAGES = ((4, 1), (7, 2), (10, 3), (12, 4), (14, 5), (16, 6))
NT = (((1,), (1,)), ((), ()))
TN = (((0,), (0,)), ((), ()))


def kernel(
    tokens,
    og, gate, up, codes, scales, zeros, amap, omap,
    gate_out, up_out, ain_out, aout_out,
    buf, w, cbuf, sc_v, ze_v, gate_v, up_v, am_v, om_v, og_v,
    hid, f1, f2, acc,
    p_src, p_dst, r0, s1, s2, s3, s4, fin, ad_mine, ad_peer,
    load_sem, code_sem, local_sem, ssem, sib_ssem, plane_sem, half_sem, near_sem, far_sem, sib_rsem, own_rsem,
    small_ssem, small_rsem,
):
    dp = lax.axis_index("dp")
    f = lax.axis_index("fsdp")
    c = lax.rem(f, 2)
    y = lax.rem(lax.div(f, 2), 4)
    x = lax.rem(lax.div(f, 8), 4)
    z = lax.div(f, 32)
    a = y + c * (x - y)
    b = x + c * (y - x)
    o = 1 - c

    def chip(px, py, pz, core):
        return (dp, ((pz * 4 + px) * 4 + py) * 2 + core)

    def neighbour(da, dz, db, core=None):
        pa, pz, pb = lax.rem(a + da, 4), lax.rem(z + dz, 4), lax.rem(b + db, 4)
        return chip(pb + c * (pa - pb), pa + c * (pb - pa), pz, c if core is None else core)

    sibling = (dp, f + 1 - 2 * c)
    partner = (1 - dp, f)

    def slot(da, dz, db):
        return lax.rem(z + dz, 4) * 16 + lax.rem(a + da, 4) * 4 + lax.rem(b + db, 4)

    def pair(da, dz):
        return lax.rem(dz, 4) * 4 + lax.rem(da, 4)

    me = slot(0, 0, 0)
    me_other = z * 16 + b * 4 + a

    bar = pltpu.get_barrier_semaphore()
    peers = [neighbour(1, 0, 0), neighbour(3, 0, 0)]
    peers += [neighbour(0, 1, 0), neighbour(0, 3, 0)]
    peers += [neighbour(0, 0, 1), neighbour(0, 0, 3)]
    peers += [neighbour(1, 0, 0, o), neighbour(3, 0, 0, o)]
    peers += [sibling, partner]
    for peer in peers:
        pl.semaphore_signal(bar, inc=1, device_id=peer, device_id_type=MESH)

    sems = (0, 0, 0, 1, 2, 3, 3)
    pairs = ((og, og_v), (gate, gate_v), (up, up_v), (amap, am_v), (omap, om_v), (scales, sc_v), (zeros, ze_v))
    loads = [pltpu.make_async_copy(p[0], p[1], load_sem.at[i]) for i, p in zip(sems, pairs)]
    for load in loads:
        load.start()

    def code_load(ch):
        return pltpu.make_async_copy(
            codes.at[:, pl.ds(pl.multiple_of(ch * 1024, 1024), 1024)], cbuf.at[ch], code_sem.at[ch // 4]
        )

    for ch in range(8):
        code_load(ch).start()

    def remote(src, dst, s_sem, r_sem, dev):
        return pltpu.make_async_remote_copy(
            src_ref=src, dst_ref=dst, send_sem=s_sem, recv_sem=r_sem, device_id=dev, device_id_type=MESH
        )

    def small(src, dst, i, dev):
        return remote(src, dst, small_ssem, small_rsem.at[i], dev)

    def own_rows(h):
        return og.at[pl.ds(pl.multiple_of(h * 256, 256), 256)]

    a_up, a_down = neighbour(1, 0, 0), neighbour(3, 0, 0)
    b_up, b_down = neighbour(0, 0, 1), neighbour(0, 0, 3)
    z_up, z_down = neighbour(0, 1, 0), neighbour(0, 3, 0)

    def send_own_z(src, k):
        for i, dev in ((3, z_up), (2, z_down)):
            remote(src, buf.at[c, me, k], ssem, half_sem.at[i * 2 + k], dev).start()

    pl.semaphore_wait(bar, len(peers))

    def wait_slots(n, sem):
        remote(buf.at[c, 0:n], buf.at[c, 0:n], ssem, sem, sibling).wait_recv()

    def wait_half(i, k):
        remote(buf.at[c, 0, k], buf.at[c, 0, k], ssem, half_sem.at[i * 2 + k], sibling).wait_recv()

    def send_whole(s, sem, dev):
        remote(buf.at[c, s], buf.at[c, s], ssem, sem, dev).start()

    def send_half(s, k, sem, dev):
        remote(buf.at[c, s, k], buf.at[c, s, k], ssem, sem, dev).start()

    def send_sib(s, da, dz):
        remote(buf.at[c, s], buf.at[c, s], sib_ssem, sib_rsem.at[pair(da, dz)], sibling).start()

    def send_b(da, dz, s):
        send_whole(s, near_sem.at[pair(da, dz)], b_up)
        send_whole(s, near_sem.at[pair(da, dz)], b_down)

    def send_z(da, s):
        send_whole(s, plane_sem.at[pair(da, 3)], z_up)
        send_whole(s, plane_sem.at[pair(da, 1)], z_down)

    def send_a(dz, s):
        send_whole(s, plane_sem.at[pair(3, dz)], a_up)
        send_whole(s, plane_sem.at[pair(1, dz)], a_down)

    sib_own_c = remote(own_rows(c), buf.at[c, me, c], sib_ssem, own_rsem.at[0], sibling)
    sib_own_o = remote(own_rows(o), buf.at[o, me_other, c], sib_ssem, own_rsem.at[1], sibling)
    sib_own_o.start()
    send_own_z(own_rows(c), c)
    for i, h, place_of, dev in (
        (1, c, me, a_up),
        (0, c, me, a_down),
        (1, o, me_other, neighbour(0, 0, 1, o)),
        (0, o, me_other, neighbour(0, 0, 3, o)),
    ):
        remote(own_rows(h), buf.at[h, place_of, c], ssem, half_sem.at[i * 2 + c], dev).start()
    local = [
        pltpu.make_async_copy(own_rows(c), buf.at[c, me, c], local_sem.at[0]),
        pltpu.make_async_copy(own_rows(o), buf.at[o, me_other, c], local_sem.at[1]),
    ]
    for copy in local:
        copy.start()
    sib_own_c.start()

    def partial_sums(h):
        rows = pl.ds(pl.multiple_of(h * 256, 256), 256)
        g = gate_v[rows, :].astype(F32)
        u = up_v[rows, :].astype(F32)
        sig = 1.0 / (1.0 + jnp.exp(-g))
        silu = g * sig
        hid[rows, :] = (silu * u).astype(BF16)
        f1[rows, :] = silu
        f2[rows, :] = u * sig * (1.0 + g * (1.0 - sig))
        p_src[h, 0:16, :] = lax.dot_general(am_v[...], hid[rows, :], NT, preferred_element_type=F32)
        p_src[h, 16:32, :] = lax.dot_general(om_v[...], og_v[rows, :], NT, preferred_element_type=F32)

    pltpu.make_async_copy(w.at[0:5], w.at[0:5], load_sem.at[0]).wait()
    loads[3].wait()
    loads[4].wait()
    partial_sums(o)
    small(p_src.at[o], p_dst, 0, sibling).start()
    remote(own_rows(o), buf.at[c, me, o], sib_ssem, own_rsem.at[1], sibling).wait_recv()
    send_own_z(buf.at[c, me, o], o)
    local[0].wait()
    send_b(0, 0, me)

    def place(s):
        da = sum(jnp.where(s == i, v[0], 0) for i, v in enumerate(ORDER) if v[0])
        dz = sum(jnp.where(s == i, v[1], 0) for i, v in enumerate(ORDER) if v[1])
        return da, dz

    def plane(s):
        da, dz = place(s)
        p = slot(da, dz, 0)
        along_a = lax.rem(dz, 2) == 0
        one, three = da == 1, da == 3
        own_a = jnp.logical_and(lax.rem(da, 2) == 1, dz == 0)
        own_z = jnp.logical_and(da == 0, lax.rem(dz, 2) == 1)

        @pl.when(jnp.logical_not(jnp.logical_or(own_a, own_z)))
        def _():
            wait_slots(1, plane_sem.at[pair(da, dz)])

        @pl.when(own_a)
        def _():
            pl.when(one)(lambda: wait_half(0, 0))
            pl.when(three)(lambda: wait_half(1, 1))

        @pl.when(along_a)
        def _():
            pl.when(one)(lambda: send_half(p, 0, plane_sem.at[pair(2, dz)], a_down))
            pl.when(three)(lambda: send_half(p, 1, plane_sem.at[pair(2, dz)], a_up))

        @pl.when(own_a)
        def _():
            pl.when(one)(lambda: wait_half(0, 1))
            pl.when(three)(lambda: wait_half(1, 0))

        @pl.when(own_z)
        def _():
            pl.when(dz == 1)(lambda: wait_half(2, o))
            pl.when(dz == 3)(lambda: wait_half(3, c))

        @pl.when(jnp.logical_and(da == 0, dz == 2))
        def _():
            send_a(dz, p)

        send_b(da, dz, p)
        send_sib(p, da, dz)

    def z_sends(s):
        @pl.when(s == Z_HALVES[0])
        def _():
            wait_half(2, c)
            send_half(slot(0, 1, 0), c, plane_sem.at[pair(0, 2)], z_down)

        @pl.when(s == Z_HALVES[1])
        def _():
            wait_half(3, o)
            send_half(slot(0, 3, 0), o, plane_sem.at[pair(0, 2)], z_up)

        for at, which in Z_SENDS:

            @pl.when(s == at)
            def _(which=which):
                send_z(which, slot(which, 0, 0))

        for at, which in Z_FAR:

            @pl.when(s == at)
            def _(which=which):
                p = slot(which, 0, 2)
                send_whole(p, far_sem.at[pair(which, 3)], z_up)
                send_whole(p, far_sem.at[pair(which, 1)], z_down)

    def cross1(s):
        da, dz = place(s)
        wait_slots(2, near_sem.at[pair(da, dz)])
        by_z = functools.reduce(jnp.logical_or, [da == which for _, which in Z_FAR])
        along_b = jnp.logical_not(jnp.logical_and(by_z, lax.rem(dz, 2) == 1))
        for db, k, dev in ((1, 0, b_down), (3, 1, b_up)):
            p = slot(da, dz, db)

            @pl.when(along_b)
            def _(p=p, k=k, dev=dev):
                send_half(p, k, far_sem.at[pair(da, dz)], dev)

            send_sib(p, da, dz)

    def cross2(s):
        da, dz = place(s)
        wait_slots(1, far_sem.at[pair(da, dz)])
        send_sib(slot(da, dz, 2), da, dz)

    def multiply(h, dz, pa):
        pz = lax.rem(z + dz, 4)
        first = pz * 16 + pa * 4
        lhs = jnp.concatenate([buf[h, first + i, k] for i in range(4) for k in range(2)], axis=1)
        rhs = jnp.concatenate([w[pz * 16 + (1 - h) * (i * 4 + pa) + h * (pa * 4 + i)] for i in range(4)], axis=1)
        total = lax.dot_general(lhs, rhs, NT, preferred_element_type=F32)
        acc[h] += total

    def multiply_own(s):
        da, dz = place(s)

        multiply(c, dz, lax.rem(a + da, 4))

    def multiply_sib(s):
        da, dz = place(s)
        pa = lax.rem(b + da, 4)

        def wait_sib(n):
            slots = buf.at[o, 0:n]
            remote(slots, slots, sib_ssem, sib_rsem.at[pair(da, dz)], sibling).wait_recv()

        @pl.when(s == 0)
        def _():
            local[1].wait()
            remote(own_rows(o), buf.at[o, me_other, o], sib_ssem, own_rsem.at[0], sibling).wait_recv()
            wait_sib(3)

        @pl.when(s > 0)
        def _():
            wait_sib(4)

        multiply(o, dz, pa)

    def dequantize(ch):
        @pl.when(ch % 4 == 0)
        def _():
            pltpu.make_async_copy(cbuf.at[0:4], cbuf.at[0:4], code_sem.at[ch // 4]).wait()

        @pl.loop(0, 4)
        def _(i):
            for g in range(2):
                rows = pl.ds(g * 128, 128)
                word = cbuf[ch, rows, pl.ds(pl.multiple_of(i * 256, 256), 256)]
                j = ch * 4 + i
                for part, level in ((0, word), (1, lax.shift_right_logical(word, 4))):
                    col = pl.ds(pl.multiple_of((j + 32 * part) * 256, 256), 256)
                    level = jnp.bitwise_and(level, 15)
                    value = sc_v[g : g + 1, col] * (level - ze_v[g : g + 1, col]).astype(F32)
                    w[j + 32 * part, rows, :] = value.astype(BF16)

    def along_x(d):
        return chip(lax.rem(x + d, 4), y, z, c)

    def along_y(d):
        return chip(x, lax.rem(y + d, 4), z, c)

    def along_z(d):
        return chip(x, y, lax.rem(z + d, 4), c)

    def all_to_all(src, dst, base, way):
        return [small(src(d), dst, base, way(d)) for d in (1, 2, 3)]

    def scatter_x():
        return all_to_all(lambda d: r0.at[lax.rem(x + d, 4)], s1.at[x], 1, along_x)

    def sum_z():
        return all_to_all(lambda d: s2.at[z], s2.at[z], 2, along_z)

    def sum_y():
        return all_to_all(lambda d: s3.at[y], s3.at[y], 3, along_y)

    def gather_x():
        return all_to_all(lambda d: s4.at[x], s4.at[x], 4, along_x)

    def share():
        return small(fin.at[c], fin.at[c], 5, sibling)

    def swap():
        return small(ad_mine, ad_peer, 6, partner)

    def begin(copies):
        for copy in copies:
            copy.start()

    def end(ref, i):
        small(ref.at[0:3], ref.at[0:3], i, sibling).wait_recv()

    def four(ref):
        return ((ref[0] + ref[1]) + ref[2]) + ref[3]

    def stage1():
        small(p_src.at[o], p_dst, 0, sibling).wait_recv()
        for i in range(4):
            rows = pl.ds(i * 8, 8)
            r0[i] = p_src[c, rows, :] + p_dst[rows, :]
        s1[x] = r0[x]
        begin(scatter_x())

    def stage2():
        end(s1, 1)
        s2[z] = four(s1)
        begin(sum_z())

    def stage3():
        end(s2, 2)
        s3[y] = four(s2)
        begin(sum_y())

    def stage4():
        end(s3, 3)
        s4[x] = four(s3)
        begin(gather_x())

    def stage5():
        end(s4, 4)
        for i in range(4):
            fin[c, pl.ds(i * 8, 8), :] = s4[i]
        share().start()

    def stage6():
        share().wait_recv()
        ain = None
        aout = None
        for h in range(2):
            rows = pl.ds(h * 256, 256)
            left = fin[h, 0:16, :].astype(BF16)
            right = fin[h, 16:32, :].astype(BF16)
            acc[h] += SCALE * lax.dot_general(right, am_v[...], TN, preferred_element_type=F32)
            p1 = jnp.dot(right, hid[rows, :], preferred_element_type=F32)
            p2 = jnp.dot(left, og_v[rows, :], preferred_element_type=F32)
            ain = p1 if ain is None else ain + p1
            aout = p2 if aout is None else aout + p2
        ad_mine[:, 0:256] = (SCALE / tokens) * ain
        ad_mine[:, 256:384] = (SCALE / tokens) * aout
        swap().start()

    def stage7():
        swap().wait_recv()
        ain_out[...] = ad_mine[:, 0:256] + ad_peer[:, 0:256]
        aout_out[...] = ad_mine[:, 256:384] + ad_peer[:, 256:384]

    partial_sums(c)
    acc[...] = jnp.zeros_like(acc)
    pltpu.make_async_copy(w.at[0:2], w.at[0:2], load_sem.at[3]).wait()
    pl.loop(0, EARLY)(dequantize)

    stages = (stage1, stage2, stage3, stage4, stage5, stage6, stage7)

    last = STEPS + LAG1 - 1

    def run(do, first, stop):
        lax.fori_loop(jnp.maximum(first, 0), stop, lambda i, _: do(i), None)

    @pl.loop(1, last + 2)
    def _(s):
        for at, stage in STAGES:
            pl.when(s == at)(stages[stage - 1])

        early = jnp.logical_and(s >= CROSS_FIRST[0], s < CROSS_FIRST[1])

        @pl.when(jnp.logical_and(s < STEPS, jnp.logical_not(early)))
        def _():
            plane(s)

        @pl.when(jnp.logical_and(s >= LAG1, s < STEPS + LAG1))
        def _():
            cross1(s - LAG1)

        z_sends(s)

        @pl.when(early)
        def _():
            plane(s)

        @pl.when(s <= 8 - EARLY)
        def _():
            dequantize(s + EARLY - 1)

        first = jnp.where(s <= SOONER[1], s - LAG_SIB, s - LAG_SIB + 1)
        stop = jnp.where(s < SOONER[1], s - LAG_SIB + 1, s - LAG_SIB + 2)
        run(multiply_sib, first, jnp.where(s > last, STEPS, stop))

        run(cross2, jnp.where(s > last, STEPS, s - LAG2), jnp.where(s < last, s - LAG2 + 1, STEPS))

        first = jnp.where(s <= SOONER[0], s - LAG_OWN, s - LAG_OWN + 1)
        stop = jnp.where(s < SOONER[0], s - LAG_OWN + 1, s - LAG_OWN + 2)
        run(multiply_own, jnp.where(s > last, STEPS, first), jnp.where(s < last, stop, STEPS))

    stage7()

    for h in range(2):
        rows = pl.ds(h * 256, 256)
        gh = acc[h]
        gate_out[rows, :] = (gh * f2[rows, :]).astype(BF16)
        up_out[rows, :] = (gh * f1[rows, :]).astype(BF16)

    remote(f1.at[0:184], f1.at[0:184], small_ssem, own_rsem.at[0], sibling).wait_send()
    remote(buf.at[0, 0:63], buf.at[0, 0:63], ssem, own_rsem.at[0], sibling).wait_send()
    remote(buf.at[0], buf.at[0], sib_ssem, own_rsem.at[0], sibling).wait_send()


def hand_over(*refs):
    n = len(refs) // 2
    copies = [pltpu.make_async_copy(refs[i], refs[n + i], refs[-1].at[i]) for i in range(n)]
    for copy in copies:
        copy.start()
    for copy in copies:
        copy.wait()


def local(og, gate, up, codes, scales, zeros, amap, omap):
    rows, cols = og.shape
    hidden = gate.shape[1]
    tokens = rows * lax.axis_size("dp")
    anywhere = pl.BlockSpec(memory_space=pl.ANY)
    dma = pltpu.SemaphoreType.DMA
    shapes = (
        jax.ShapeDtypeStruct((rows, hidden), BF16),
        jax.ShapeDtypeStruct((rows, hidden), BF16),
        jax.ShapeDtypeStruct((16, hidden), F32),
        jax.ShapeDtypeStruct((16, cols), F32),
    )
    results = pl.pallas_call(
        functools.partial(kernel, tokens),
        out_shape=tuple(pltpu.VMEM(v.shape, v.dtype) for v in shapes),
        in_specs=[anywhere] * 8,
        out_specs=[pl.BlockSpec(memory_space=pltpu.VMEM)] * 4,
        scratch_shapes=[
            pltpu.VMEM((2, 64, 2, 256, 128), BF16),
            pltpu.VMEM((64, 256, 256), BF16),
            pltpu.VMEM((8, 256, 1024), jnp.int32),
            pltpu.VMEM((2, 16384), F32),
            pltpu.VMEM((2, 16384), jnp.int32),
            pltpu.VMEM((512, 256), BF16),
            pltpu.VMEM((512, 256), BF16),
            pltpu.VMEM((16, 256), BF16),
            pltpu.VMEM((16, 128), BF16),
            pltpu.VMEM((512, 128), BF16),
            pltpu.VMEM((512, 256), BF16),
            pltpu.VMEM((512, 256), F32),
            pltpu.VMEM((512, 256), F32),
            pltpu.VMEM((2, 256, 256), F32),
            pltpu.VMEM((2, 32, 256), F32),
            pltpu.VMEM((32, 256), F32),
            pltpu.VMEM((4, 8, 256), F32),
            pltpu.VMEM((4, 8, 256), F32),
            pltpu.VMEM((4, 8, 256), F32),
            pltpu.VMEM((4, 8, 256), F32),
            pltpu.VMEM((4, 8, 256), F32),
            pltpu.VMEM((2, 32, 256), F32),
            pltpu.VMEM((16, 384), F32),
            pltpu.VMEM((16, 384), F32),
            dma((4,)),
            dma((2,)),
            dma((2,)),
            dma,
            dma,
            dma((16,)),
            dma((8,)),
            dma((16,)),
            dma((16,)),
            dma((16,)),
            dma((2,)),
            dma,
            dma((7,)),
        ],
        compiler_params=pltpu.CompilerParams(
            collective_id=0, has_side_effects=True, vmem_limit_bytes=58 * 2**20
        ),
        name="backward",
    )(og, gate, up, codes, scales, zeros, amap, omap)
    return pl.pallas_call(
        hand_over,
        out_shape=shapes,
        in_specs=[pl.BlockSpec(memory_space=pltpu.VMEM)] * 4,
        out_specs=[anywhere] * 4,
        scratch_shapes=[dma((4,))],
        name="hand_over",
    )(*(pltpu.with_memory_space_constraint(v, pltpu.VMEM) for v in results))


def solution(mesh):
    in_specs = (
        P("dp", "fsdp"),
        P("dp", "fsdp"),
        P("dp", "fsdp"),
        P("fsdp", None),
        P("fsdp", None),
        P("fsdp", None),
        P(None, "fsdp"),
        P(None, "fsdp"),
    )
    out_specs = (P("dp", "fsdp"), P("dp", "fsdp"), P(None, "fsdp"), P(None, "fsdp"))
    return jax.shard_map(local, mesh=mesh, in_specs=in_specs, out_specs=out_specs, check_vma=False)
```

```python
import functools

import jax
import jax.numpy as jnp
from jax import lax
from jax.experimental import pallas as pl
from jax.experimental.pallas import tpu as pltpu
from jax.sharding import PartitionSpec as P

MESH = pl.DeviceIdType.MESH
F32 = jnp.float32
BF16 = jnp.bfloat16
SCALE = 2.0
LAG1, LAG2, LAG_OWN, LAG_SIB = 3, 6, 7, 8
STEPS = 16
ORDER = ((0, 0), (1, 0), (3, 0), (0, 1), (0, 3), (2, 0), (0, 2), (1, 1), (1, 3), (1, 2), (3, 2), (3, 1), (3, 3), (2, 2), (2, 1), (2, 3))
Z_SENDS = ((3, 1), (8, 3), (10, 2))
Z_HALVES = (2, 3)
Z_FAR = ((12, 2),)
SOONER = (11, 17)
CROSS_FIRST = (3, 12)
EARLY = 6
STAGES = ((4, 1), (7, 2), (10, 3), (12, 4), (14, 5), (16, 6))
NT = (((1,), (1,)), ((), ()))
TN = (((0,), (0,)), ((), ()))


def kernel(
    tokens,
    og, gate, up, codes, scales, zeros, amap, omap,
    gate_out, up_out, ain_out, aout_out,
    buf, w, cbuf, sc_v, ze_v, gate_v, up_v, am_v, om_v, og_v,
    hid, f1, f2, acc,
    p_src, p_dst, r0, s1, s2, s3, s4, fin, ad_mine, ad_peer,
    load_sem, code_sem, local_sem, ssem, sib_ssem, plane_sem, half_sem, near_sem, far_sem, sib_rsem, own_rsem,
    small_ssem, small_rsem,
):
    dp = lax.axis_index("dp")
    f = lax.axis_index("fsdp")
    c = lax.rem(f, 2)
    y = lax.rem(lax.div(f, 2), 4)
    x = lax.rem(lax.div(f, 8), 4)
    z = lax.div(f, 32)
    a = y + c * (x - y)
    b = x + c * (y - x)
    o = 1 - c

    def chip(px, py, pz, core):
        return (dp, ((pz * 4 + px) * 4 + py) * 2 + core)

    def neighbour(da, dz, db, core=None):
        pa, pz, pb = lax.rem(a + da, 4), lax.rem(z + dz, 4), lax.rem(b + db, 4)
        return chip(pb + c * (pa - pb), pa + c * (pb - pa), pz, c if core is None else core)

    sibling = (dp, f + 1 - 2 * c)
    partner = (1 - dp, f)

    def slot(da, dz, db):
        return lax.rem(z + dz, 4) * 16 + lax.rem(a + da, 4) * 4 + lax.rem(b + db, 4)

    def pair(da, dz):
        return lax.rem(dz, 4) * 4 + lax.rem(da, 4)

    me = slot(0, 0, 0)
    me_other = z * 16 + b * 4 + a

    bar = pltpu.get_barrier_semaphore()
    peers = [neighbour(1, 0, 0), neighbour(3, 0, 0)]
    peers += [neighbour(0, 1, 0), neighbour(0, 3, 0)]
    peers += [neighbour(0, 0, 1), neighbour(0, 0, 3)]
    peers += [neighbour(1, 0, 0, o), neighbour(3, 0, 0, o)]
    peers += [sibling, partner]
    for peer in peers:
        pl.semaphore_signal(bar, inc=1, device_id=peer, device_id_type=MESH)

    sems = (0, 0, 0, 1, 2, 3, 3)
    pairs = ((og, og_v), (gate, gate_v), (up, up_v), (amap, am_v), (omap, om_v), (scales, sc_v), (zeros, ze_v))
    loads = [pltpu.make_async_copy(p[0], p[1], load_sem.at[i]) for i, p in zip(sems, pairs)]
    for load in loads:
        load.start()

    def code_load(ch):
        return pltpu.make_async_copy(
            codes.at[:, pl.ds(pl.multiple_of(ch * 1024, 1024), 1024)], cbuf.at[ch], code_sem.at[ch // 4]
        )

    for ch in range(8):
        code_load(ch).start()

    def remote(src, dst, s_sem, r_sem, dev):
        return pltpu.make_async_remote_copy(
            src_ref=src, dst_ref=dst, send_sem=s_sem, recv_sem=r_sem, device_id=dev, device_id_type=MESH
        )

    def small(src, dst, i, dev):
        return remote(src, dst, small_ssem, small_rsem.at[i], dev)

    def own_rows(h):
        return og.at[pl.ds(pl.multiple_of(h * 256, 256), 256)]

    a_up, a_down = neighbour(1, 0, 0), neighbour(3, 0, 0)
    b_up, b_down = neighbour(0, 0, 1), neighbour(0, 0, 3)
    z_up, z_down = neighbour(0, 1, 0), neighbour(0, 3, 0)

    def send_own_z(src, k):
        for i, dev in ((3, z_up), (2, z_down)):
            remote(src, buf.at[c, me, k], ssem, half_sem.at[i * 2 + k], dev).start()

    pl.semaphore_wait(bar, len(peers))

    def wait_slots(n, sem):
        remote(buf.at[c, 0:n], buf.at[c, 0:n], ssem, sem, sibling).wait_recv()

    def wait_half(i, k):
        remote(buf.at[c, 0, k], buf.at[c, 0, k], ssem, half_sem.at[i * 2 + k], sibling).wait_recv()

    def send_whole(s, sem, dev):
        remote(buf.at[c, s], buf.at[c, s], ssem, sem, dev).start()

    def send_half(s, k, sem, dev):
        remote(buf.at[c, s, k], buf.at[c, s, k], ssem, sem, dev).start()

    def send_sib(s, da, dz):
        remote(buf.at[c, s], buf.at[c, s], sib_ssem, sib_rsem.at[pair(da, dz)], sibling).start()

    def send_b(da, dz, s):
        send_whole(s, near_sem.at[pair(da, dz)], b_up)
        send_whole(s, near_sem.at[pair(da, dz)], b_down)

    def send_z(da, s):
        send_whole(s, plane_sem.at[pair(da, 3)], z_up)
        send_whole(s, plane_sem.at[pair(da, 1)], z_down)

    def send_a(dz, s):
        send_whole(s, plane_sem.at[pair(3, dz)], a_up)
        send_whole(s, plane_sem.at[pair(1, dz)], a_down)

    sib_own_c = remote(own_rows(c), buf.at[c, me, c], sib_ssem, own_rsem.at[0], sibling)
    sib_own_o = remote(own_rows(o), buf.at[o, me_other, c], sib_ssem, own_rsem.at[1], sibling)
    sib_own_o.start()
    send_own_z(own_rows(c), c)
    for i, h, place_of, dev in (
        (1, c, me, a_up),
        (0, c, me, a_down),
        (1, o, me_other, neighbour(0, 0, 1, o)),
        (0, o, me_other, neighbour(0, 0, 3, o)),
    ):
        remote(own_rows(h), buf.at[h, place_of, c], ssem, half_sem.at[i * 2 + c], dev).start()
    for dev in (b_up, b_down):
        remote(own_rows(c), buf.at[c, me, c], ssem, near_sem.at[pair(0, 0)], dev).start()
    local = [
        pltpu.make_async_copy(own_rows(c), buf.at[c, me, c], local_sem.at[0]),
        pltpu.make_async_copy(own_rows(o), buf.at[o, me_other, c], local_sem.at[1]),
    ]
    for copy in local:
        copy.start()
    sib_own_c.start()

    def partial_sums(h):
        rows = pl.ds(pl.multiple_of(h * 256, 256), 256)
        g = gate_v[rows, :].astype(F32)
        u = up_v[rows, :].astype(F32)
        sig = 1.0 / (1.0 + jnp.exp(-g))
        silu = g * sig
        hid[rows, :] = (silu * u).astype(BF16)
        f1[rows, :] = silu
        f2[rows, :] = u * sig * (1.0 + g * (1.0 - sig))
        p_src[h, 0:16, :] = lax.dot_general(am_v[...], hid[rows, :], NT, preferred_element_type=F32)
        p_src[h, 16:32, :] = lax.dot_general(om_v[...], og_v[rows, :], NT, preferred_element_type=F32)

    pltpu.make_async_copy(w.at[0:5], w.at[0:5], load_sem.at[0]).wait()
    loads[3].wait()
    loads[4].wait()
    partial_sums(o)
    small(p_src.at[o], p_dst, 0, sibling).start()
    remote(own_rows(o), buf.at[c, me, o], sib_ssem, own_rsem.at[1], sibling).wait_recv()
    send_own_z(buf.at[c, me, o], o)
    local[0].wait()
    for dev in (b_up, b_down):
        send_half(me, o, near_sem.at[pair(0, 0)], dev)

    def place(s):
        da = sum(jnp.where(s == i, v[0], 0) for i, v in enumerate(ORDER) if v[0])
        dz = sum(jnp.where(s == i, v[1], 0) for i, v in enumerate(ORDER) if v[1])
        return da, dz

    def plane(s):
        da, dz = place(s)
        p = slot(da, dz, 0)
        along_a = lax.rem(dz, 2) == 0
        one, three = da == 1, da == 3
        own_a = jnp.logical_and(lax.rem(da, 2) == 1, dz == 0)
        own_z = jnp.logical_and(da == 0, lax.rem(dz, 2) == 1)

        @pl.when(jnp.logical_not(jnp.logical_or(own_a, own_z)))
        def _():
            wait_slots(1, plane_sem.at[pair(da, dz)])

        @pl.when(own_a)
        def _():
            pl.when(one)(lambda: wait_half(0, 0))
            pl.when(three)(lambda: wait_half(1, 1))

        @pl.when(along_a)
        def _():
            pl.when(one)(lambda: send_half(p, 0, plane_sem.at[pair(2, dz)], a_down))
            pl.when(three)(lambda: send_half(p, 1, plane_sem.at[pair(2, dz)], a_up))

        @pl.when(own_a)
        def _():
            pl.when(one)(lambda: wait_half(0, 1))
            pl.when(three)(lambda: wait_half(1, 0))

        @pl.when(own_z)
        def _():
            pl.when(dz == 1)(lambda: wait_half(2, o))
            pl.when(dz == 3)(lambda: wait_half(3, c))

        @pl.when(jnp.logical_and(da == 0, dz == 2))
        def _():
            send_a(dz, p)

        send_b(da, dz, p)
        send_sib(p, da, dz)

    def z_sends(s):
        @pl.when(s == Z_HALVES[0])
        def _():
            wait_half(2, c)
            send_half(slot(0, 1, 0), c, plane_sem.at[pair(0, 2)], z_down)

        @pl.when(s == Z_HALVES[1])
        def _():
            wait_half(3, o)
            send_half(slot(0, 3, 0), o, plane_sem.at[pair(0, 2)], z_up)

        for at, which in Z_SENDS:

            @pl.when(s == at)
            def _(which=which):
                send_z(which, slot(which, 0, 0))

        for at, which in Z_FAR:

            @pl.when(s == at)
            def _(which=which):
                p = slot(which, 0, 2)
                send_whole(p, far_sem.at[pair(which, 3)], z_up)
                send_whole(p, far_sem.at[pair(which, 1)], z_down)

    def cross1(s):
        da, dz = place(s)
        wait_slots(2, near_sem.at[pair(da, dz)])
        by_z = functools.reduce(jnp.logical_or, [da == which for _, which in Z_FAR])
        along_b = jnp.logical_not(jnp.logical_and(by_z, lax.rem(dz, 2) == 1))
        for db, k, dev in ((1, 0, b_down), (3, 1, b_up)):
            p = slot(da, dz, db)

            @pl.when(along_b)
            def _(p=p, k=k, dev=dev):
                send_half(p, k, far_sem.at[pair(da, dz)], dev)

            send_sib(p, da, dz)

    def cross2(s):
        da, dz = place(s)
        wait_slots(1, far_sem.at[pair(da, dz)])
        send_sib(slot(da, dz, 2), da, dz)

    def multiply(h, dz, pa):
        pz = lax.rem(z + dz, 4)
        first = pz * 16 + pa * 4
        lhs = jnp.concatenate([buf[h, first + i, k] for i in range(4) for k in range(2)], axis=1)
        rhs = jnp.concatenate([w[pz * 16 + (1 - h) * (i * 4 + pa) + h * (pa * 4 + i)] for i in range(4)], axis=1)
        total = lax.dot_general(lhs, rhs, NT, preferred_element_type=F32)
        acc[h] += total

    def multiply_own(s):
        da, dz = place(s)

        multiply(c, dz, lax.rem(a + da, 4))

    def multiply_sib(s):
        da, dz = place(s)
        pa = lax.rem(b + da, 4)

        def wait_sib(n):
            slots = buf.at[o, 0:n]
            remote(slots, slots, sib_ssem, sib_rsem.at[pair(da, dz)], sibling).wait_recv()

        @pl.when(s == 0)
        def _():
            local[1].wait()
            remote(own_rows(o), buf.at[o, me_other, o], sib_ssem, own_rsem.at[0], sibling).wait_recv()
            wait_sib(3)

        @pl.when(s > 0)
        def _():
            wait_sib(4)

        multiply(o, dz, pa)

    def dequantize(ch):
        @pl.when(ch % 4 == 0)
        def _():
            pltpu.make_async_copy(cbuf.at[0:4], cbuf.at[0:4], code_sem.at[ch // 4]).wait()

        @pl.loop(0, 4)
        def _(i):
            for g in range(2):
                rows = pl.ds(g * 128, 128)
                word = cbuf[ch, rows, pl.ds(pl.multiple_of(i * 256, 256), 256)]
                j = ch * 4 + i
                for part, level in ((0, word), (1, lax.shift_right_logical(word, 4))):
                    col = pl.ds(pl.multiple_of((j + 32 * part) * 256, 256), 256)
                    level = jnp.bitwise_and(level, 15)
                    value = sc_v[g : g + 1, col] * (level - ze_v[g : g + 1, col]).astype(F32)
                    w[j + 32 * part, rows, :] = value.astype(BF16)

    def along_x(d):
        return chip(lax.rem(x + d, 4), y, z, c)

    def along_y(d):
        return chip(x, lax.rem(y + d, 4), z, c)

    def along_z(d):
        return chip(x, y, lax.rem(z + d, 4), c)

    def all_to_all(src, dst, base, way):
        return [small(src(d), dst, base, way(d)) for d in (1, 2, 3)]

    def scatter_x():
        return all_to_all(lambda d: r0.at[lax.rem(x + d, 4)], s1.at[x], 1, along_x)

    def sum_z():
        return all_to_all(lambda d: s2.at[z], s2.at[z], 2, along_z)

    def sum_y():
        return all_to_all(lambda d: s3.at[y], s3.at[y], 3, along_y)

    def gather_x():
        return all_to_all(lambda d: s4.at[x], s4.at[x], 4, along_x)

    def share():
        return small(fin.at[c], fin.at[c], 5, sibling)

    def swap():
        return small(ad_mine, ad_peer, 6, partner)

    def begin(copies):
        for copy in copies:
            copy.start()

    def end(ref, i):
        small(ref.at[0:3], ref.at[0:3], i, sibling).wait_recv()

    def four(ref):
        return ((ref[0] + ref[1]) + ref[2]) + ref[3]

    def stage1():
        small(p_src.at[o], p_dst, 0, sibling).wait_recv()
        for i in range(4):
            rows = pl.ds(i * 8, 8)
            r0[i] = p_src[c, rows, :] + p_dst[rows, :]
        s1[x] = r0[x]
        begin(scatter_x())

    def stage2():
        end(s1, 1)
        s2[z] = four(s1)
        begin(sum_z())

    def stage3():
        end(s2, 2)
        s3[y] = four(s2)
        begin(sum_y())

    def stage4():
        end(s3, 3)
        s4[x] = four(s3)
        begin(gather_x())

    def stage5():
        end(s4, 4)
        for i in range(4):
            fin[c, pl.ds(i * 8, 8), :] = s4[i]
        share().start()

    def stage6():
        share().wait_recv()
        ain = None
        aout = None
        for h in range(2):
            rows = pl.ds(h * 256, 256)
            left = fin[h, 0:16, :].astype(BF16)
            right = fin[h, 16:32, :].astype(BF16)
            acc[h] += SCALE * lax.dot_general(right, am_v[...], TN, preferred_element_type=F32)
            p1 = jnp.dot(right, hid[rows, :], preferred_element_type=F32)
            p2 = jnp.dot(left, og_v[rows, :], preferred_element_type=F32)
            ain = p1 if ain is None else ain + p1
            aout = p2 if aout is None else aout + p2
        ad_mine[:, 0:256] = (SCALE / tokens) * ain
        ad_mine[:, 256:384] = (SCALE / tokens) * aout
        swap().start()

    def stage7():
        swap().wait_recv()
        ain_out[...] = ad_mine[:, 0:256] + ad_peer[:, 0:256]
        aout_out[...] = ad_mine[:, 256:384] + ad_peer[:, 256:384]

    partial_sums(c)
    acc[...] = jnp.zeros_like(acc)
    pltpu.make_async_copy(w.at[0:2], w.at[0:2], load_sem.at[3]).wait()
    pl.loop(0, EARLY)(dequantize)

    stages = (stage1, stage2, stage3, stage4, stage5, stage6, stage7)

    last = STEPS + LAG1 - 1

    def run(do, first, stop):
        lax.fori_loop(jnp.maximum(first, 0), stop, lambda i, _: do(i), None)

    @pl.loop(1, last + 2)
    def _(s):
        for at, stage in STAGES:
            pl.when(s == at)(stages[stage - 1])

        early = jnp.logical_and(s >= CROSS_FIRST[0], s < CROSS_FIRST[1])

        @pl.when(jnp.logical_and(s < STEPS, jnp.logical_not(early)))
        def _():
            plane(s)

        @pl.when(jnp.logical_and(s >= LAG1, s < STEPS + LAG1))
        def _():
            cross1(s - LAG1)

        z_sends(s)

        @pl.when(early)
        def _():
            plane(s)

        @pl.when(s <= 8 - EARLY)
        def _():
            dequantize(s + EARLY - 1)

        first = jnp.where(s <= SOONER[1], s - LAG_SIB, s - LAG_SIB + 1)
        stop = jnp.where(s < SOONER[1], s - LAG_SIB + 1, s - LAG_SIB + 2)
        run(multiply_sib, first, jnp.where(s > last, STEPS, stop))

        run(cross2, jnp.where(s > last, STEPS, s - LAG2), jnp.where(s < last, s - LAG2 + 1, STEPS))

        first = jnp.where(s <= SOONER[0], s - LAG_OWN, s - LAG_OWN + 1)
        stop = jnp.where(s < SOONER[0], s - LAG_OWN + 1, s - LAG_OWN + 2)
        run(multiply_own, jnp.where(s > last, STEPS, first), jnp.where(s < last, stop, STEPS))

    stage7()

    for h in range(2):
        rows = pl.ds(h * 256, 256)
        gh = acc[h]
        gate_out[rows, :] = (gh * f2[rows, :]).astype(BF16)
        up_out[rows, :] = (gh * f1[rows, :]).astype(BF16)

    remote(f1.at[0:184], f1.at[0:184], small_ssem, own_rsem.at[0], sibling).wait_send()
    remote(buf.at[0, 0:63], buf.at[0, 0:63], ssem, own_rsem.at[0], sibling).wait_send()
    remote(buf.at[0], buf.at[0], sib_ssem, own_rsem.at[0], sibling).wait_send()


def hand_over(*refs):
    n = len(refs) // 2
    copies = [pltpu.make_async_copy(refs[i], refs[n + i], refs[-1].at[i]) for i in range(n)]
    for copy in copies:
        copy.start()
    for copy in copies:
        copy.wait()


def local(og, gate, up, codes, scales, zeros, amap, omap):
    rows, cols = og.shape
    hidden = gate.shape[1]
    tokens = rows * lax.axis_size("dp")
    anywhere = pl.BlockSpec(memory_space=pl.ANY)
    dma = pltpu.SemaphoreType.DMA
    shapes = (
        jax.ShapeDtypeStruct((rows, hidden), BF16),
        jax.ShapeDtypeStruct((rows, hidden), BF16),
        jax.ShapeDtypeStruct((16, hidden), F32),
        jax.ShapeDtypeStruct((16, cols), F32),
    )
    results = pl.pallas_call(
        functools.partial(kernel, tokens),
        out_shape=tuple(pltpu.VMEM(v.shape, v.dtype) for v in shapes),
        in_specs=[anywhere] * 8,
        out_specs=[pl.BlockSpec(memory_space=pltpu.VMEM)] * 4,
        scratch_shapes=[
            pltpu.VMEM((2, 64, 2, 256, 128), BF16),
            pltpu.VMEM((64, 256, 256), BF16),
            pltpu.VMEM((8, 256, 1024), jnp.int32),
            pltpu.VMEM((2, 16384), F32),
            pltpu.VMEM((2, 16384), jnp.int32),
            pltpu.VMEM((512, 256), BF16),
            pltpu.VMEM((512, 256), BF16),
            pltpu.VMEM((16, 256), BF16),
            pltpu.VMEM((16, 128), BF16),
            pltpu.VMEM((512, 128), BF16),
            pltpu.VMEM((512, 256), BF16),
            pltpu.VMEM((512, 256), F32),
            pltpu.VMEM((512, 256), F32),
            pltpu.VMEM((2, 256, 256), F32),
            pltpu.VMEM((2, 32, 256), F32),
            pltpu.VMEM((32, 256), F32),
            pltpu.VMEM((4, 8, 256), F32),
            pltpu.VMEM((4, 8, 256), F32),
            pltpu.VMEM((4, 8, 256), F32),
            pltpu.VMEM((4, 8, 256), F32),
            pltpu.VMEM((4, 8, 256), F32),
            pltpu.VMEM((2, 32, 256), F32),
            pltpu.VMEM((16, 384), F32),
            pltpu.VMEM((16, 384), F32),
            dma((4,)),
            dma((2,)),
            dma((2,)),
            dma,
            dma,
            dma((16,)),
            dma((8,)),
            dma((16,)),
            dma((16,)),
            dma((16,)),
            dma((2,)),
            dma,
            dma((7,)),
        ],
        compiler_params=pltpu.CompilerParams(
            collective_id=0, has_side_effects=True, vmem_limit_bytes=58 * 2**20
        ),
        name="backward",
    )(og, gate, up, codes, scales, zeros, amap, omap)
    return pl.pallas_call(
        hand_over,
        out_shape=shapes,
        in_specs=[pl.BlockSpec(memory_space=pltpu.VMEM)] * 4,
        out_specs=[anywhere] * 4,
        scratch_shapes=[dma((4,))],
        name="hand_over",
    )(*(pltpu.with_memory_space_constraint(v, pltpu.VMEM) for v in results))


def solution(mesh):
    in_specs = (
        P("dp", "fsdp"),
        P("dp", "fsdp"),
        P("dp", "fsdp"),
        P("fsdp", None),
        P("fsdp", None),
        P("fsdp", None),
        P(None, "fsdp"),
        P(None, "fsdp"),
    )
    out_specs = (P("dp", "fsdp"), P("dp", "fsdp"), P(None, "fsdp"), P(None, "fsdp"))
    return jax.shard_map(local, mesh=mesh, in_specs=in_specs, out_specs=out_specs, check_vma=False)
```

```python
import functools

import jax
import jax.numpy as jnp
from jax import lax
from jax.experimental import pallas as pl
from jax.experimental.pallas import tpu as pltpu
from jax.sharding import PartitionSpec as P

MESH = pl.DeviceIdType.MESH
F32 = jnp.float32
BF16 = jnp.bfloat16
SCALE = 2.0
LAG1, LAG2, LAG_OWN, LAG_SIB = 3, 6, 7, 8
STEPS = 16
ORDER = ((0, 0), (1, 0), (3, 0), (0, 1), (0, 3), (2, 0), (0, 2), (1, 1), (1, 3), (1, 2), (3, 2), (3, 1), (3, 3), (2, 2), (2, 1), (2, 3))
Z_SENDS = ((3, 1), (8, 3), (10, 2))
Z_HALVES = (2, 3)
Z_FAR = ((12, 2),)
SOONER = (11, 17)
CROSS_FIRST = (3, 12)
EARLY = 6
STAGES = ((4, 1), (7, 2), (10, 3), (12, 4), (14, 5), (16, 6))
NT = (((1,), (1,)), ((), ()))
TN = (((0,), (0,)), ((), ()))


def kernel(
    tokens,
    og, gate, up, codes, scales, zeros, amap, omap,
    gate_out, up_out, ain_out, aout_out,
    buf, w, cbuf, sc_v, ze_v, gate_v, up_v, am_v, om_v, og_v,
    hid, f1, f2, acc,
    p_src, p_dst, r0, s1, s2, s3, s4, fin, ad_mine, ad_peer,
    load_sem, code_sem, local_sem, ssem, sib_ssem, plane_sem, half_sem, near_sem, far_sem, sib_rsem, own_rsem,
    small_ssem, small_rsem,
):
    dp = lax.axis_index("dp")
    f = lax.axis_index("fsdp")
    c = lax.rem(f, 2)
    y = lax.rem(lax.div(f, 2), 4)
    x = lax.rem(lax.div(f, 8), 4)
    z = lax.div(f, 32)
    a = y + c * (x - y)
    b = x + c * (y - x)
    o = 1 - c

    def chip(px, py, pz, core):
        return (dp, ((pz * 4 + px) * 4 + py) * 2 + core)

    def neighbour(da, dz, db, core=None):
        pa, pz, pb = lax.rem(a + da, 4), lax.rem(z + dz, 4), lax.rem(b + db, 4)
        return chip(pb + c * (pa - pb), pa + c * (pb - pa), pz, c if core is None else core)

    sibling = (dp, f + 1 - 2 * c)
    partner = (1 - dp, f)

    def slot(da, dz, db):
        return lax.rem(z + dz, 4) * 16 + lax.rem(a + da, 4) * 4 + lax.rem(b + db, 4)

    def pair(da, dz):
        return lax.rem(dz, 4) * 4 + lax.rem(da, 4)

    me = slot(0, 0, 0)
    me_other = z * 16 + b * 4 + a

    bar = pltpu.get_barrier_semaphore()
    peers = [neighbour(1, 0, 0), neighbour(3, 0, 0)]
    peers += [neighbour(0, 1, 0), neighbour(0, 3, 0)]
    peers += [neighbour(0, 0, 1), neighbour(0, 0, 3)]
    peers += [neighbour(1, 0, 0, o), neighbour(3, 0, 0, o)]
    peers += [sibling, partner]
    for peer in peers:
        pl.semaphore_signal(bar, inc=1, device_id=peer, device_id_type=MESH)

    sems = (0, 0, 0, 1, 2, 3, 3)
    pairs = ((og, og_v), (gate, gate_v), (up, up_v), (amap, am_v), (omap, om_v), (scales, sc_v), (zeros, ze_v))
    loads = [pltpu.make_async_copy(p[0], p[1], load_sem.at[i]) for i, p in zip(sems, pairs)]
    for load in loads:
        load.start()

    def code_load(ch):
        return pltpu.make_async_copy(
            codes.at[:, pl.ds(pl.multiple_of(ch * 1024, 1024), 1024)], cbuf.at[ch], code_sem.at[ch // 4]
        )

    for ch in range(8):
        code_load(ch).start()

    def remote(src, dst, s_sem, r_sem, dev):
        return pltpu.make_async_remote_copy(
            src_ref=src, dst_ref=dst, send_sem=s_sem, recv_sem=r_sem, device_id=dev, device_id_type=MESH
        )

    def small(src, dst, i, dev):
        return remote(src, dst, small_ssem, small_rsem.at[i], dev)

    def own_rows(h):
        return og.at[pl.ds(pl.multiple_of(h * 256, 256), 256)]

    a_up, a_down = neighbour(1, 0, 0), neighbour(3, 0, 0)
    b_up, b_down = neighbour(0, 0, 1), neighbour(0, 0, 3)
    z_up, z_down = neighbour(0, 1, 0), neighbour(0, 3, 0)

    def send_own_z(src, k):
        for i, dev in ((3, z_up), (2, z_down)):
            remote(src, buf.at[c, me, k], ssem, half_sem.at[i * 2 + k], dev).start()

    pl.semaphore_wait(bar, len(peers))

    def wait_slots(n, sem):
        remote(buf.at[c, 0:n], buf.at[c, 0:n], ssem, sem, sibling).wait_recv()

    def wait_half(i, k):
        remote(buf.at[c, 0, k], buf.at[c, 0, k], ssem, half_sem.at[i * 2 + k], sibling).wait_recv()

    def send_whole(s, sem, dev):
        remote(buf.at[c, s], buf.at[c, s], ssem, sem, dev).start()

    def send_half(s, k, sem, dev):
        remote(buf.at[c, s, k], buf.at[c, s, k], ssem, sem, dev).start()

    def send_sib(s, da, dz):
        remote(buf.at[c, s], buf.at[c, s], sib_ssem, sib_rsem.at[pair(da, dz)], sibling).start()

    def send_b(da, dz, s):
        send_whole(s, near_sem.at[pair(da, dz)], b_up)
        send_whole(s, near_sem.at[pair(da, dz)], b_down)

    def send_z(da, s):
        send_whole(s, plane_sem.at[pair(da, 3)], z_up)
        send_whole(s, plane_sem.at[pair(da, 1)], z_down)

    def send_a(dz, s):
        send_whole(s, plane_sem.at[pair(3, dz)], a_up)
        send_whole(s, plane_sem.at[pair(1, dz)], a_down)

    sib_own_c = remote(own_rows(c), buf.at[c, me, c], sib_ssem, own_rsem.at[0], sibling)
    sib_own_o = remote(own_rows(o), buf.at[o, me_other, c], sib_ssem, own_rsem.at[1], sibling)
    sib_own_o.start()
    send_own_z(own_rows(c), c)
    for i, h, place_of, dev in (
        (1, c, me, a_up),
        (0, c, me, a_down),
        (1, o, me_other, neighbour(0, 0, 1, o)),
        (0, o, me_other, neighbour(0, 0, 3, o)),
    ):
        remote(own_rows(h), buf.at[h, place_of, c], ssem, half_sem.at[i * 2 + c], dev).start()
    local = [
        pltpu.make_async_copy(own_rows(c), buf.at[c, me, c], local_sem.at[0]),
        pltpu.make_async_copy(own_rows(o), buf.at[o, me_other, c], local_sem.at[1]),
    ]
    for copy in local:
        copy.start()
    sib_own_c.start()

    def partial_sums(h):
        rows = pl.ds(pl.multiple_of(h * 256, 256), 256)
        g = gate_v[rows, :].astype(F32)
        u = up_v[rows, :].astype(F32)
        sig = 1.0 / (1.0 + jnp.exp(-g))
        silu = g * sig
        hid[rows, :] = (silu * u).astype(BF16)
        f1[rows, :] = silu
        f2[rows, :] = u * sig * (1.0 + g * (1.0 - sig))
        p_src[h, 0:16, :] = lax.dot_general(am_v[...], hid[rows, :], NT, preferred_element_type=F32)
        p_src[h, 16:32, :] = lax.dot_general(om_v[...], og_v[rows, :], NT, preferred_element_type=F32)

    pltpu.make_async_copy(w.at[0:5], w.at[0:5], load_sem.at[0]).wait()
    loads[3].wait()
    loads[4].wait()
    partial_sums(o)
    small(p_src.at[o], p_dst, 0, sibling).start()
    remote(own_rows(o), buf.at[c, me, o], sib_ssem, own_rsem.at[1], sibling).wait_recv()
    send_own_z(buf.at[c, me, o], o)
    local[0].wait()
    send_b(0, 0, me)

    def place(s):
        da = sum(jnp.where(s == i, v[0], 0) for i, v in enumerate(ORDER) if v[0])
        dz = sum(jnp.where(s == i, v[1], 0) for i, v in enumerate(ORDER) if v[1])
        return da, dz

    def plane(s):
        da, dz = place(s)
        p = slot(da, dz, 0)
        along_a = lax.rem(dz, 2) == 0
        one, three = da == 1, da == 3
        own_a = jnp.logical_and(lax.rem(da, 2) == 1, dz == 0)
        own_z = jnp.logical_and(da == 0, lax.rem(dz, 2) == 1)

        @pl.when(jnp.logical_not(jnp.logical_or(own_a, own_z)))
        def _():
            wait_slots(1, plane_sem.at[pair(da, dz)])

        @pl.when(own_a)
        def _():
            pl.when(one)(lambda: wait_half(0, 0))
            pl.when(three)(lambda: wait_half(1, 1))

        @pl.when(along_a)
        def _():
            pl.when(one)(lambda: send_half(p, 0, plane_sem.at[pair(2, dz)], a_down))
            pl.when(three)(lambda: send_half(p, 1, plane_sem.at[pair(2, dz)], a_up))

        @pl.when(own_a)
        def _():
            pl.when(one)(lambda: wait_half(0, 1))
            pl.when(three)(lambda: wait_half(1, 0))

        @pl.when(own_z)
        def _():
            pl.when(dz == 1)(lambda: wait_half(2, o))
            pl.when(dz == 3)(lambda: wait_half(3, c))

        @pl.when(jnp.logical_and(da == 0, dz == 2))
        def _():
            send_a(dz, p)

        send_b(da, dz, p)
        send_sib(p, da, dz)

    def z_sends(s):
        @pl.when(s == Z_HALVES[0])
        def _():
            wait_half(2, c)
            send_half(slot(0, 1, 0), c, plane_sem.at[pair(0, 2)], z_down)

        @pl.when(s == Z_HALVES[1])
        def _():
            wait_half(3, o)
            send_half(slot(0, 3, 0), o, plane_sem.at[pair(0, 2)], z_up)

        for at, which in Z_SENDS:

            @pl.when(s == at)
            def _(which=which):
                send_z(which, slot(which, 0, 0))

        for at, which in Z_FAR:

            @pl.when(s == at)
            def _(which=which):
                p = slot(which, 0, 2)
                send_whole(p, far_sem.at[pair(which, 3)], z_up)
                send_whole(p, far_sem.at[pair(which, 1)], z_down)

    def cross1(s):
        da, dz = place(s)
        wait_slots(2, near_sem.at[pair(da, dz)])
        by_z = functools.reduce(jnp.logical_or, [da == which for _, which in Z_FAR])
        along_b = jnp.logical_not(jnp.logical_and(by_z, lax.rem(dz, 2) == 1))
        for db, k, dev in ((1, 0, b_down), (3, 1, b_up)):
            p = slot(da, dz, db)

            @pl.when(along_b)
            def _(p=p, k=k, dev=dev):
                send_half(p, k, far_sem.at[pair(da, dz)], dev)

            send_sib(p, da, dz)

    def cross2(s):
        da, dz = place(s)
        wait_slots(1, far_sem.at[pair(da, dz)])
        send_sib(slot(da, dz, 2), da, dz)

    def multiply(h, dz, pa):
        pz = lax.rem(z + dz, 4)
        first = pz * 16 + pa * 4
        lhs = jnp.concatenate([buf[h, first + i, k] for i in range(4) for k in range(2)], axis=1)
        rhs = jnp.concatenate([w[pz * 16 + (1 - h) * (i * 4 + pa) + h * (pa * 4 + i)] for i in range(4)], axis=1)
        total = lax.dot_general(lhs, rhs, NT, preferred_element_type=F32)
        acc[h] += total

    def multiply_own(s):
        da, dz = place(s)

        multiply(c, dz, lax.rem(a + da, 4))

    def multiply_sib(s):
        da, dz = place(s)
        pa = lax.rem(b + da, 4)

        def wait_sib(n):
            slots = buf.at[o, 0:n]
            remote(slots, slots, sib_ssem, sib_rsem.at[pair(da, dz)], sibling).wait_recv()

        @pl.when(s == 0)
        def _():
            local[1].wait()
            remote(own_rows(o), buf.at[o, me_other, o], sib_ssem, own_rsem.at[0], sibling).wait_recv()
            wait_sib(3)

        @pl.when(s > 0)
        def _():
            wait_sib(4)

        multiply(o, dz, pa)

    def dequantize(ch):
        @pl.when(ch % 4 == 0)
        def _():
            pltpu.make_async_copy(cbuf.at[0:4], cbuf.at[0:4], code_sem.at[ch // 4]).wait()

        @pl.loop(0, 4)
        def _(i):
            for g in range(2):
                rows = pl.ds(g * 128, 128)
                word = cbuf[ch, rows, pl.ds(pl.multiple_of(i * 256, 256), 256)]
                j = ch * 4 + i
                for part, level in ((0, word), (1, lax.shift_right_logical(word, 4))):
                    col = pl.ds(pl.multiple_of((j + 32 * part) * 256, 256), 256)
                    level = jnp.bitwise_and(level, 15)
                    value = sc_v[g : g + 1, col] * (level - ze_v[g : g + 1, col]).astype(F32)
                    w[j + 32 * part, rows, :] = value.astype(BF16)

    def along_x(d):
        return chip(lax.rem(x + d, 4), y, z, c)

    def along_y(d):
        return chip(x, lax.rem(y + d, 4), z, c)

    def along_z(d):
        return chip(x, y, lax.rem(z + d, 4), c)

    def all_to_all(src, dst, base, way):
        return [small(src(d), dst, base, way(d)) for d in (1, 2, 3)]

    def scatter_x():
        return all_to_all(lambda d: r0.at[lax.rem(x + d, 4)], s1.at[x], 1, along_x)

    def sum_z():
        return all_to_all(lambda d: s2.at[z], s2.at[z], 2, along_z)

    def sum_y():
        return all_to_all(lambda d: s3.at[y], s3.at[y], 3, along_y)

    def gather_x():
        return all_to_all(lambda d: s4.at[x], s4.at[x], 4, along_x)

    def share():
        return small(fin.at[c], fin.at[c], 5, sibling)

    def swap():
        return small(ad_mine, ad_peer, 6, partner)

    def begin(copies):
        for copy in copies:
            copy.start()

    def end(ref, i):
        small(ref.at[0:3], ref.at[0:3], i, sibling).wait_recv()

    def four(ref):
        return ((ref[0] + ref[1]) + ref[2]) + ref[3]

    def stage1():
        small(p_src.at[o], p_dst, 0, sibling).wait_recv()
        for i in range(4):
            rows = pl.ds(i * 8, 8)
            r0[i] = p_src[c, rows, :] + p_dst[rows, :]
        s1[x] = r0[x]
        begin(scatter_x())

    def stage2():
        end(s1, 1)
        s2[z] = four(s1)
        begin(sum_z())

    def stage3():
        end(s2, 2)
        s3[y] = four(s2)
        begin(sum_y())

    def stage4():
        end(s3, 3)
        s4[x] = four(s3)
        begin(gather_x())

    def stage5():
        end(s4, 4)
        for i in range(4):
            fin[c, pl.ds(i * 8, 8), :] = s4[i]
        share().start()

    def stage6():
        share().wait_recv()
        ain = None
        aout = None
        for h in range(2):
            rows = pl.ds(h * 256, 256)
            left = fin[h, 0:16, :].astype(BF16)
            right = fin[h, 16:32, :].astype(BF16)
            acc[h] += SCALE * lax.dot_general(right, am_v[...], TN, preferred_element_type=F32)
            p1 = jnp.dot(right, hid[rows, :], preferred_element_type=F32)
            p2 = jnp.dot(left, og_v[rows, :], preferred_element_type=F32)
            ain = p1 if ain is None else ain + p1
            aout = p2 if aout is None else aout + p2
        ad_mine[:, 0:256] = (SCALE / tokens) * ain
        ad_mine[:, 256:384] = (SCALE / tokens) * aout
        swap().start()

    def stage7():
        swap().wait_recv()
        ain_out[...] = ad_mine[:, 0:256] + ad_peer[:, 0:256]
        aout_out[...] = ad_mine[:, 256:384] + ad_peer[:, 256:384]

    partial_sums(c)
    acc[...] = jnp.zeros_like(acc)
    pltpu.make_async_copy(w.at[0:2], w.at[0:2], load_sem.at[3]).wait()
    pl.loop(0, EARLY)(dequantize)

    stages = (stage1, stage2, stage3, stage4, stage5, stage6, stage7)

    last = STEPS + LAG1 - 1

    def run(do, first, stop):
        lax.fori_loop(jnp.maximum(first, 0), stop, lambda i, _: do(i), None)

    @pl.loop(1, last + 2)
    def _(s):
        for at, stage in STAGES:
            pl.when(s == at)(stages[stage - 1])

        early = jnp.logical_and(s >= CROSS_FIRST[0], s < CROSS_FIRST[1])

        @pl.when(jnp.logical_and(s < STEPS, jnp.logical_not(early)))
        def _():
            plane(s)

        @pl.when(jnp.logical_and(s >= LAG1, s < STEPS + LAG1))
        def _():
            cross1(s - LAG1)

        z_sends(s)

        @pl.when(early)
        def _():
            plane(s)

        @pl.when(s <= 8 - EARLY)
        def _():
            dequantize(s + EARLY - 1)

        first = jnp.where(s <= SOONER[1], s - LAG_SIB, s - LAG_SIB + 1)
        stop = jnp.where(s < SOONER[1], s - LAG_SIB + 1, s - LAG_SIB + 2)
        run(multiply_sib, first, jnp.where(s > last, STEPS, stop))

        run(cross2, jnp.where(s > last, STEPS, s - LAG2), jnp.where(s < last, s - LAG2 + 1, STEPS))

        first = jnp.where(s <= SOONER[0], s - LAG_OWN, s - LAG_OWN + 1)
        stop = jnp.where(s < SOONER[0], s - LAG_OWN + 1, s - LAG_OWN + 2)
        run(multiply_own, jnp.where(s > last, STEPS, first), jnp.where(s < last, stop, STEPS))

    stage7()

    for h in range(2):
        rows = pl.ds(h * 256, 256)
        gh = acc[h]
        gate_out[rows, :] = (gh * f2[rows, :]).astype(BF16)
        up_out[rows, :] = (gh * f1[rows, :]).astype(BF16)

    remote(f1.at[0:184], f1.at[0:184], small_ssem, own_rsem.at[0], sibling).wait_send()
    remote(buf.at[0, 0:63], buf.at[0, 0:63], ssem, own_rsem.at[0], sibling).wait_send()
    remote(buf.at[0], buf.at[0], sib_ssem, own_rsem.at[0], sibling).wait_send()


def hand_over(*refs):
    n = len(refs) // 2
    copies = [pltpu.make_async_copy(refs[i], refs[n + i], refs[-1].at[i]) for i in range(n)]
    for copy in copies:
        copy.start()
    for copy in copies:
        copy.wait()


def local(og, gate, up, codes, scales, zeros, amap, omap):
    rows, cols = og.shape
    hidden = gate.shape[1]
    tokens = rows * lax.axis_size("dp")
    anywhere = pl.BlockSpec(memory_space=pl.ANY)
    dma = pltpu.SemaphoreType.DMA
    shapes = (
        jax.ShapeDtypeStruct((rows, hidden), BF16),
        jax.ShapeDtypeStruct((rows, hidden), BF16),
        jax.ShapeDtypeStruct((16, hidden), F32),
        jax.ShapeDtypeStruct((16, cols), F32),
    )
    results = pl.pallas_call(
        functools.partial(kernel, tokens),
        out_shape=tuple(pltpu.VMEM(v.shape, v.dtype) for v in shapes),
        in_specs=[anywhere] * 8,
        out_specs=[pl.BlockSpec(memory_space=pltpu.VMEM)] * 4,
        scratch_shapes=[
            pltpu.VMEM((2, 64, 2, 256, 128), BF16),
            pltpu.VMEM((64, 256, 256), BF16),
            pltpu.VMEM((8, 256, 1024), jnp.int32),
            pltpu.VMEM((2, 16384), F32),
            pltpu.VMEM((2, 16384), jnp.int32),
            pltpu.VMEM((512, 256), BF16),
            pltpu.VMEM((512, 256), BF16),
            pltpu.VMEM((16, 256), BF16),
            pltpu.VMEM((16, 128), BF16),
            pltpu.VMEM((512, 128), BF16),
            pltpu.VMEM((512, 256), BF16),
            pltpu.VMEM((512, 256), F32),
            pltpu.VMEM((512, 256), F32),
            pltpu.VMEM((2, 256, 256), F32),
            pltpu.VMEM((2, 32, 256), F32),
            pltpu.VMEM((32, 256), F32),
            pltpu.VMEM((4, 8, 256), F32),
            pltpu.VMEM((4, 8, 256), F32),
            pltpu.VMEM((4, 8, 256), F32),
            pltpu.VMEM((4, 8, 256), F32),
            pltpu.VMEM((4, 8, 256), F32),
            pltpu.VMEM((2, 32, 256), F32),
            pltpu.VMEM((16, 384), F32),
            pltpu.VMEM((16, 384), F32),
            dma((4,)),
            dma((2,)),
            dma((2,)),
            dma,
            dma,
            dma((16,)),
            dma((8,)),
            dma((16,)),
            dma((16,)),
            dma((16,)),
            dma((2,)),
            dma,
            dma((7,)),
        ],
        compiler_params=pltpu.CompilerParams(
            collective_id=0, has_side_effects=True, vmem_limit_bytes=58 * 2**20
        ),
        name="backward",
    )(og, gate, up, codes, scales, zeros, amap, omap)
    return pl.pallas_call(
        hand_over,
        out_shape=shapes,
        in_specs=[pl.BlockSpec(memory_space=pltpu.VMEM)] * 4,
        out_specs=[anywhere] * 4,
        scratch_shapes=[dma((4,))],
        name="hand_over",
    )(*(pltpu.with_memory_space_constraint(v, pltpu.VMEM) for v in results))


def solution(mesh):
    in_specs = (
        P("dp", "fsdp"),
        P("dp", "fsdp"),
        P("dp", "fsdp"),
        P("fsdp", None),
        P("fsdp", None),
        P("fsdp", None),
        P(None, "fsdp"),
        P(None, "fsdp"),
    )
    out_specs = (P("dp", "fsdp"), P("dp", "fsdp"), P(None, "fsdp"), P(None, "fsdp"))
    return jax.shard_map(local, mesh=mesh, in_specs=in_specs, out_specs=out_specs, check_vma=False)
```
